768 devices in a mesh: stream: 192 (over z_hi, x, y, core), span: 4 (over z_lo).
Axes of the slice: x: 4, y: 8, z: 12 (z_hi: 3, z_lo: 4; z = z_hi * 4 + z_lo), core: 2. Of those that a mesh axis runs over, the one named last changes fastest.
Arguments:
- source: float32 [3072, 24, 512], P('stream', None, 'span'), may hold values from -24 to 24
- geometry: bfloat16 [6, 3072, 24, 512], P(None, 'stream', None, 'span'), may hold values from -1.68 to 36, as said below
Outputs:
- solution_field: float32 [3072, 24, 512], P('stream', None, 'span')
- residual: float32 [3072, 24, 512], P('stream', None, 'span')
The draws below stay inside these ranges and needn't reach their ends.
Inputs may be any that keep to these rules, and one draw needn't show every extreme that they name: `geometry`: at every point the three leading factors are positive and each exceeds the sum of the magnitudes of the two coupling factors of its row.
All inputs are finite; a program needn't handle non-finite values.
Results may differ from the reference program's by a relative error of at most 0.024.
Values sent between devices are 32-bit elements; how exact they have to be, the bound alone decides.
A program may use at most 32 MiB of HBM per device.

```python
import jax
import jax.numpy as jnp
import numpy as np
from jax import lax

NODES = 8
EX = 2
WALL_ELEMENTS = 3
ITERS = 3
STREAM_ELEMENTS = 384
SPAN_ELEMENTS = 64
NX = 3072
NY = 24
NZ = 512


def draw_source(key, part):
    key = jax.random.fold_in(key, 11)
    noise_key, scale_key = jax.random.split(key, 2)
    xgrid = jnp.arange(NX, dtype=jnp.float32)[:, None, None] / NX
    gradient_trend = jnp.exp(jnp.log(3.0) * xgrid)
    fluctuation = jax.random.truncated_normal(noise_key, -4.0, 4.0, (NX, NY, NZ), jnp.float32)
    roughness = jax.random.uniform(scale_key, (NX, NY, NZ), jnp.float32, 0.5, 2.0)
    result = gradient_trend * fluctuation * roughness
    return result.astype(jnp.float32)


def draw_geometry(key, part):
    key = jax.random.fold_in(key, 23)
    diagonal_key, coupling_key, phase_key = jax.random.split(key, 3)
    phases = jax.random.uniform(phase_key, (2,), jnp.float32, 0.0, 1.0)
    xgrid = jnp.mod(jnp.arange(NX, dtype=jnp.float32) / NX + phases[0], 1.0)
    zgrid = jnp.mod(jnp.arange(NZ, dtype=jnp.float32) / NZ + phases[1], 1.0)
    stiffness_trend = jnp.exp(jnp.log(4.0) * xgrid[None, :, None, None] + jnp.log(1.5) * zgrid[None, None, None, :])
    diagonal = jnp.exp(jax.random.uniform(diagonal_key, (3, NX, NY, NZ), jnp.float32, jnp.log(0.6), jnp.log(2.4)))
    coupling = jax.random.uniform(coupling_key, (3, NX, NY, NZ), jnp.float32, -0.28, 0.28)
    return (jnp.concatenate([diagonal, coupling], axis=0) * stiffness_trend).astype(jnp.bfloat16)


def setup_inputs(seed: int = 0) -> dict:
    arg_keys = jax.random.split(jax.random.key(seed), 3)
    return {
        "source": draw_source(jax.random.fold_in(arg_keys[2], 71), 0),
        "geometry": draw_geometry(jax.random.fold_in(arg_keys[2], 71), 0),
    }


def gll_tables():
    gll_points = np.array([-1.0, -0.8717401485096066, -0.5917001814331423, -0.2092992179024789, 0.2092992179024789, 0.5917001814331423, 0.8717401485096066, 1.0])
    quadrature_weight = np.array([1.0 / 28.0, 0.2107042271435061, 0.3411226924835044, 0.4124587946587038, 0.4124587946587038, 0.3411226924835044, 0.2107042271435061, 1.0 / 28.0])
    barycentric = np.array([1.0 / np.prod([gll_points[j] - gll_points[k] for k in range(8) if k != j]) for j in range(8)])
    derivative = np.zeros((8, 8))
    for j in range(8):
        for k in range(8):
            if j != k:
                derivative[j, k] = barycentric[k] / barycentric[j] / (gll_points[j] - gll_points[k])
    for j in range(8):
        derivative[j, j] = -np.sum(derivative[j])
    return quadrature_weight, derivative


def boundary_half_parts(elements):
    pattern = np.ones(NODES)
    pattern[0] = 0.5
    pattern[NODES - 1] = 0.5
    return np.tile(pattern, elements)


def wall_table(count):
    table = np.ones(count)
    table[0] = 0.0
    table[count - 1] = 0.0
    return table


def pair_faces(interior, lower_plane, upper_plane, axis_dim):
    extent = interior.shape
    elements = extent[axis_dim] // NODES
    blocks = interior.reshape(extent[:axis_dim] + (elements, NODES) + extent[axis_dim + 1:])
    first_planes = lax.index_in_dim(blocks, 0, axis_dim + 1, keepdims=False)
    last_planes = lax.index_in_dim(blocks, NODES - 1, axis_dim + 1, keepdims=False)
    next_planes = jnp.concatenate([lax.slice_in_dim(first_planes, 1, elements, axis=axis_dim), upper_plane], axis=axis_dim)
    face_sums = last_planes + next_planes
    prev_planes = jnp.concatenate([lower_plane + lax.slice_in_dim(first_planes, 0, 1, axis=axis_dim), lax.slice_in_dim(face_sums, 0, elements - 1, axis=axis_dim)], axis=axis_dim)
    middle = lax.slice_in_dim(blocks, 1, NODES - 1, axis=axis_dim + 1)
    joined = jnp.concatenate([jnp.expand_dims(prev_planes, axis_dim + 1), middle, jnp.expand_dims(face_sums, axis_dim + 1)], axis=axis_dim + 1)
    return joined.reshape(extent)


def derivative_along(values, matrix, axis_dim):
    extent = values.shape
    elements = extent[axis_dim] // NODES
    blocks = values.reshape(extent[:axis_dim] + (elements, NODES) + extent[axis_dim + 1:])
    if axis_dim == 0:
        derived = jnp.einsum('ij,ejyz->eiyz', matrix, blocks, precision=lax.Precision.HIGHEST)
    elif axis_dim == 1:
        derived = jnp.einsum('ij,xejz->xeiz', matrix, blocks, precision=lax.Precision.HIGHEST)
    else:
        derived = jnp.einsum('ij,xyej->xyei', matrix, blocks, precision=lax.Precision.HIGHEST)
    return derived.reshape(extent)


def local_stiffness(values, metric_half, matrix, quad_x, quad_y, spanwise_quadrature):
    metric = metric_half.astype(jnp.float32)
    gradients = [derivative_along(values, matrix, axis_dim) for axis_dim in range(3)]
    weight = quad_x[:, None, None] * quad_y[None, :, None] * spanwise_quadrature[None, None, :]
    couplings = ((0, 3, 4), (3, 1, 5), (4, 5, 2))
    total = jnp.zeros(values.shape, jnp.float32)
    for axis_dim in range(3):
        components = couplings[axis_dim]
        flux = weight * (metric[components[0]] * gradients[0] + metric[components[1]] * gradients[1] + metric[components[2]] * gradients[2])
        total = total + derivative_along(flux, matrix.T, axis_dim)
    return total


def reference(source, geometry):
    quadrature_weight, derivative_table = gll_tables()
    matrix = jnp.asarray(derivative_table, dtype=jnp.float32)
    slab_rows = EX * NODES
    quad_x = jnp.asarray(np.tile(quadrature_weight, EX), dtype=jnp.float32)
    quad_y = jnp.asarray(np.tile(quadrature_weight, WALL_ELEMENTS), dtype=jnp.float32)
    spanwise_quadrature = jnp.asarray(np.tile(quadrature_weight, SPAN_ELEMENTS), dtype=jnp.float32)
    half_parts = jnp.asarray(boundary_half_parts(STREAM_ELEMENTS), dtype=jnp.float32)[:, None, None] * jnp.asarray(boundary_half_parts(WALL_ELEMENTS), dtype=jnp.float32)[None, :, None] * jnp.asarray(boundary_half_parts(SPAN_ELEMENTS), dtype=jnp.float32)[None, None, :]
    wall_mask = jnp.asarray(wall_table(NY), dtype=jnp.float32)[None, :, None]

    def assemble(values):
        values = pair_faces(values, values[-1:], values[0:1], 0)
        values = pair_faces(values, jnp.zeros_like(values[:, 0:1]), jnp.zeros_like(values[:, 0:1]), 1)
        return pair_faces(values, values[:, :, -1:], values[:, :, 0:1], 2)

    def apply_operator(values):
        def one_slab(slab_index):
            slab_start = slab_index * slab_rows
            slab_values = lax.dynamic_slice_in_dim(values, slab_start, slab_rows, 0)
            slab_metric = lax.dynamic_slice_in_dim(geometry, slab_start, slab_rows, 1)
            return local_stiffness(slab_values, slab_metric, matrix, quad_x, quad_y, spanwise_quadrature)

        stiffness = lax.map(one_slab, jnp.arange(NX // slab_rows, dtype=jnp.int32)).reshape(values.shape)
        return wall_mask * assemble(stiffness)

    def weighted_inner(first_field, second_field):
        return jnp.sum(first_field * second_field * half_parts)

    right_side = wall_mask * assemble(source)
    solution_field = jnp.zeros_like(right_side)
    residual = right_side
    direction = right_side
    norm_now = weighted_inner(residual, residual)
    for iteration in range(ITERS):
        applied = apply_operator(direction)
        step_size = norm_now / weighted_inner(direction, applied)
        solution_field = solution_field + step_size * direction
        residual = residual - step_size * applied
        norm_next = weighted_inner(residual, residual)
        direction = residual + (norm_next / norm_now) * direction
        norm_now = norm_next
    return solution_field, residual
```

```python
import functools

import jax
import jax.numpy as jnp
import numpy as np
from jax import lax
from jax.experimental import pallas as pl
from jax.experimental.pallas import tpu as pltpu
from jax.sharding import PartitionSpec as P

MESH = pl.DeviceIdType.MESH
NODES = 8
EX = 2
EY = 3
LANES = 128
ROUNDS = 4
HIGHEST = lax.Precision.HIGHEST
Z_HI, X, Y, CORES, Z_LO = 3, 4, 8, 2, 4
Z = Z_HI * Z_LO


def gll_tables():
    points = np.array(
        [
            -1.0,
            -0.8717401485096066,
            -0.5917001814331423,
            -0.2092992179024789,
            0.2092992179024789,
            0.5917001814331423,
            0.8717401485096066,
            1.0,
        ]
    )
    weights = np.array(
        [
            1.0 / 28.0,
            0.2107042271435061,
            0.3411226924835044,
            0.4124587946587038,
            0.4124587946587038,
            0.3411226924835044,
            0.2107042271435061,
            1.0 / 28.0,
        ]
    )
    barycentric = np.array(
        [
            1.0 / np.prod([points[j] - points[k] for k in range(8) if k != j])
            for j in range(8)
        ]
    )
    derivative = np.zeros((8, 8))
    for j in range(8):
        for k in range(8):
            if j != k:
                derivative[j, k] = barycentric[k] / barycentric[j] / (points[j] - points[k])
    for j in range(8):
        derivative[j, j] = -np.sum(derivative[j])
    return weights, derivative


WEIGHTS, DERIVATIVE = gll_tables()


def constants():
    half = np.ones(NODES)
    half[0] = half[-1] = 0.5
    copies = LANES // NODES
    blocks = np.kron(np.eye(copies), DERIVATIVE)
    weight = WEIGHTS[:, None] * np.tile(WEIGHTS, copies)[None, :]
    halves = half[:, None] * np.tile(half, copies)[None, :]
    return np.concatenate([blocks, blocks.T, weight, halves]).astype(np.float32)


def neighbours(count_s, count_p):
    s, p = lax.axis_index("stream"), lax.axis_index("span")
    down, up = lax.rem(s + count_s - 1, count_s), lax.rem(s + 1, count_s)
    left, right = lax.rem(p + count_p - 1, count_p), lax.rem(p + 1, count_p)
    return s, p, down, up, left, right


def column_peers(s, p):
    core, z_hi = lax.rem(s, CORES), s // (X * Y * CORES)
    base = s - core - z_hi * (X * Y * CORES)
    z = z_hi * Z_LO + p
    peers = []
    for dz in range(Z):
        for dc in range(CORES):
            if dz or dc:
                other = lax.rem(z + dz, Z)
                c = lax.rem(core + dc, CORES)
                peers.append((base + (other // Z_LO) * (X * Y * CORES) + c, lax.rem(other, Z_LO)))
    return peers


def plane_peers(s, p):
    core, row = lax.rem(s, CORES), s // CORES
    y, x, z_hi = lax.rem(row, Y), lax.rem(row // Y, X), row // (X * Y)
    peers = []
    for dx in range(X):
        for dy in range(Y):
            if dx or dy:
                there = (z_hi * X + lax.rem(x + dx, X)) * Y + lax.rem(y + dy, Y)
                peers.append((there * CORES + core, p))
    return peers


def along_x(parts, matrix):
    even = [parts[j] + parts[7 - j] for j in range(4)]
    odd = [parts[j] - parts[7 - j] for j in range(4)]
    low, high = [None] * 4, [None] * 4
    for i in range(4):
        a = sum(odd[j] * float(0.5 * (matrix[i, j] - matrix[i, 7 - j])) for j in range(4))
        b = sum(even[j] * float(0.5 * (matrix[i, j] + matrix[i, 7 - j])) for j in range(4))
        low[i], high[i] = b + a, a - b
    return low + high[::-1]


def kernel(
    count_s,
    count_p,
    source_hbm,
    geometry_hbm,
    constant_hbm,
    solution_ref,
    residual_ref,
    source,
    geometry,
    constant,
    metric,
    fields,
    partial,
    planes,
    packs,
    packed,
    grad1,
    grad2,
    row1,
    row2,
    column,
    plane,
    load_sem,
    send_sem,
    recv_sem,
    sum_send,
    sum_recv,
):
    s, p, down, up, left, right = neighbours(count_s, count_p)
    halo = [(down, p), (up, p), (s, left), (s, right)]
    halo += [(down, left), (down, right), (up, left), (up, right)]
    in_column, in_plane = column_peers(s, p), plane_peers(s, p)

    loads = [
        pltpu.make_async_copy(source_hbm, source, load_sem.at[0]),
        pltpu.make_async_copy(constant_hbm, constant, load_sem.at[1]),
        pltpu.make_async_copy(geometry_hbm, geometry, load_sem.at[2]),
    ]
    barrier = pltpu.get_barrier_semaphore()
    for peer in halo + in_column + in_plane:
        pl.semaphore_signal(barrier, inc=1, device_id=peer, device_id_type=MESH)
    for load in loads:
        load.start()

    lane = lax.broadcasted_iota(jnp.int32, (NODES, LANES), 1)
    sub = lax.broadcasted_iota(jnp.int32, (NODES, LANES), 0)
    node = lax.rem(lane, NODES)
    from_right = (node == NODES - 1) & (lane != LANES - 1)
    from_left = (node == 0) & (lane != 0)

    def assemble(values, k):
        tiles = [[values[x, 8 * e : 8 * e + 8] for e in range(EY)] for x in range(EX * NODES)]
        for e in range(EY):
            joined = tiles[NODES - 1][e] + tiles[NODES][e]
            tiles[NODES - 1][e] = tiles[NODES][e] = joined
        for x in range(EX * NODES):
            if x == NODES:
                for e in range(EY):
                    partial[k, x, 8 * e : 8 * e + 8, :] = tiles[NODES - 1][e]
                tiles[x] = tiles[NODES - 1]
                continue
            row = tiles[x]
            new = list(row)
            for e in range(EY - 1):
                new[e] = new[e] + jnp.where(sub == 7, pltpu.roll(row[e + 1], 7, 0), 0.0)
                new[e + 1] = new[e + 1] + jnp.where(sub == 0, pltpu.roll(row[e], 1, 0), 0.0)
            new[0] = jnp.where(sub == 0, 0.0, new[0])
            new[-1] = jnp.where(sub == 7, 0.0, new[-1])
            for e in range(EY):
                t = new[e]
                t = (
                    t
                    + jnp.where(from_right, pltpu.roll(t, LANES - 1, 1), 0.0)
                    + jnp.where(from_left, pltpu.roll(t, 1, 1), 0.0)
                )
                new[e] = t
                partial[k, x, 8 * e : 8 * e + 8, :] = t
            tiles[x] = new
        pack = jnp.zeros((NODES, LANES), jnp.float32)
        for x in range(EX * NODES):
            for e in range(EY):
                j = x * EY + e
                pack = jnp.where(lane // 2 == j, pltpu.roll(tiles[x][e], 2 * j + 1, 1), pack)
        packed[k] = pack

    last = EX * NODES - 1

    def exchanges(k):
        sources = [partial.at[k, 0], partial.at[k, last]] + [packed.at[k]] * 6
        targets = [planes.at[k, 1], planes.at[k, 0]]
        targets += [packs.at[k, i] for i in (1, 0, 5, 4, 3, 2)]
        slots = [1, 0, 3, 2, 7, 6, 5, 4]
        return [
            pltpu.make_async_remote_copy(
                src_ref=a,
                dst_ref=b,
                send_sem=send_sem.at[k, i],
                recv_sem=recv_sem.at[k, slots[i]],
                device_id=peer,
                device_id_type=MESH,
            )
            for i, (a, b, peer) in enumerate(zip(sources, targets, halo))
        ]

    def finish(k, want_norm):
        edge = EY * 2 * last
        low, high = lane < 2 * EY, (lane >= edge) & (lane < edge + 2 * EY)

        def with_corners(face, below, above):
            return (
                face
                + jnp.where(low, pltpu.roll(below, LANES - edge, 1), 0.0)
                + jnp.where(high, pltpu.roll(above, edge, 1), 0.0)
            )

        minus = with_corners(packs[k, 0], packs[k, 2], packs[k, 4])
        plus = with_corners(packs[k, 1], packs[k, 3], packs[k, 5])
        faces = jnp.where(
            lax.rem(lane, 2) == 0, pltpu.roll(plus, LANES - 1, 1), pltpu.roll(minus, 1, 1)
        )
        ends = (lane == 0) | (lane == LANES - 1)
        inner = jnp.zeros((NODES, LANES), jnp.float32)
        outer = jnp.zeros((NODES, LANES), jnp.float32)
        for x in range(EX * NODES):
            for e in range(EY):
                j = x * EY + e
                t = partial[k, x, 8 * e : 8 * e + 8, :]
                if x == 0:
                    t = t + planes[k, 0, 8 * e : 8 * e + 8, :]
                if x == last:
                    t = t + planes[k, 1, 8 * e : 8 * e + 8, :]
                t = t + jnp.where(ends, pltpu.roll(faces, LANES - 2 * j - 1, 1), 0.0)
                fields[k, x, 8 * e : 8 * e + 8, :] = t
                if want_norm:
                    if x % NODES in (0, NODES - 1):
                        outer = outer + t * t
                    else:
                        inner = inner + t * t
        return (inner + 0.5 * outer) * constant[2 * LANES + NODES : 2 * LANES + 2 * NODES, :]

    def fluxes(k):
        values = fields[k]
        flat = values.reshape(EX * NODES * EY * NODES, LANES)
        grad2[...] = jnp.dot(
            flat, constant[LANES : 2 * LANES, :], precision=HIGHEST
        ).reshape(values.shape)
        for r in range(3):
            grad1[16 * r : 16 * r + 16] = jnp.dot(
                constant[0:LANES, :], flat[LANES * r : LANES * r + LANES], precision=HIGHEST
            ).reshape(16, NODES, LANES)
        energy = jnp.zeros((NODES, LANES), jnp.float32)
        flux0 = {}
        for ex in range(EX):
            for e in range(EY):
                rows = slice(8 * e, 8 * e + 8)
                g0 = along_x([fields[k, ex * 8 + i, rows, :] for i in range(8)], DERIVATIVE)
                for i in range(8):
                    x = ex * 8 + i
                    j = x * EY + e
                    m = [metric[c, x, rows, :] for c in range(6)]
                    g1, g2 = grad1[j], grad2[x, rows, :]
                    f0 = m[0] * g0[i] + m[3] * g1 + m[4] * g2
                    f1 = m[3] * g0[i] + m[1] * g1 + m[5] * g2
                    f2 = m[4] * g0[i] + m[5] * g1 + m[2] * g2
                    energy = energy + (f0 * g0[i] + f1 * g1 + f2 * g2)
                    flux0[x, e] = f0
                    grad1[j] = f1
                    grad2[x, rows, :] = f2
        return flux0, energy

    def divergence(flux0):
        along2 = jnp.dot(
            grad2[...].reshape(EX * NODES * EY * NODES, LANES),
            constant[0:LANES, :],
            precision=HIGHEST,
        ).reshape(EX * NODES, EY * NODES, LANES)
        for r in range(3):
            grad1[16 * r : 16 * r + 16] = jnp.dot(
                constant[LANES : 2 * LANES, :],
                grad1[16 * r : 16 * r + 16].reshape(LANES, LANES),
                precision=HIGHEST,
            ).reshape(16, NODES, LANES)
        total = {}
        for ex in range(EX):
            for e in range(EY):
                back = along_x([flux0[ex * 8 + i, e] for i in range(8)], DERIVATIVE.T)
                for i in range(8):
                    x = ex * 8 + i
                    total[x, e] = (
                        back[i] + grad1[x * EY + e] + along2[x, 8 * e : 8 * e + 8]
                    )
        return jnp.stack(
            [
                jnp.concatenate([total[x, e] for e in range(EY)], axis=0)
                for x in range(EX * NODES)
            ]
        )

    def fold(tile, width):
        shift = LANES // 2
        while shift >= width:
            tile = tile + pltpu.roll(tile, shift, 1)
            shift //= 2
        return tile

    loads[0].wait()
    assemble(source[...], 0)
    pl.semaphore_wait(barrier, len(halo) + len(in_column) + len(in_plane))
    flight = exchanges(0)
    for copy in flight:
        copy.start()
    loads[1].wait()
    loads[2].wait()
    weight = constant[2 * LANES : 2 * LANES + NODES, :]
    for c in range(6):
        for x in range(EX * NODES):
            scaled = geometry[c, x].astype(jnp.float32)
            for e in range(EY):
                metric[c, x, 8 * e : 8 * e + 8, :] = scaled[8 * e : 8 * e + 8] * (
                    weight * float(WEIGHTS[x % NODES])
                )

    moments = []
    for k in range(ROUNDS - 1):
        for copy in flight:
            copy.wait_recv()
        moments.append(finish(k, True))
        flux0, energy = fluxes(k)
        moments.append(energy)
        if k == ROUNDS - 2:
            packed_moments = jnp.where(
                lane < 96, fold(moments[4], 32), fold(moments[5], 32)
            )
            for i in range(4):
                packed_moments = jnp.where(
                    lane // 16 == i, fold(moments[i], 16), packed_moments
                )
            row1[...] = jnp.sum(packed_moments, axis=0, keepdims=True)
            for i, peer in enumerate(in_column):
                pltpu.make_async_remote_copy(
                    src_ref=row1,
                    dst_ref=column.at[pl.ds(i, 1)],
                    send_sem=sum_send.at[0],
                    recv_sem=sum_recv.at[0],
                    device_id=peer,
                    device_id_type=MESH,
                ).start()
        for copy in flight:
            copy.wait_send()
        assemble(divergence(flux0), k + 1)
        flight = exchanges(k + 1)
        for copy in flight:
            copy.start()

    def whole(buffer, i, peer):
        return pltpu.make_async_remote_copy(
            src_ref=buffer,
            dst_ref=buffer,
            send_sem=sum_send.at[i],
            recv_sem=sum_recv.at[i],
            device_id=peer,
            device_id_type=MESH,
        )

    whole(column, 0, in_column[0]).wait_recv()
    row2[...] = row1[...] + jnp.sum(column[...], axis=0, keepdims=True)
    for i, peer in enumerate(in_plane):
        pltpu.make_async_remote_copy(
            src_ref=row2,
            dst_ref=plane.at[pl.ds(i, 1)],
            send_sem=sum_send.at[1],
            recv_sem=sum_recv.at[1],
            device_id=peer,
            device_id_type=MESH,
        ).start()
    for copy in flight:
        copy.wait_recv()
    finish(ROUNDS - 1, False)
    whole(plane, 1, in_plane[0]).wait_recv()
    total = row2[...] + jnp.sum(plane[...], axis=0, keepdims=True)
    group = lax.broadcasted_iota(jnp.int32, (1, LANES), 1)
    bounds = [0, 16, 32, 48, 64, 96, 128]
    m = [
        jnp.sum(
            jnp.where((group >= bounds[i]) & (group < bounds[i + 1]), total, 0.0),
            axis=1,
            keepdims=True,
        )
        for i in range(6)
    ]
    alpha0 = m[0] / m[1]
    norm1 = alpha0 * alpha0 * m[2] - m[0]
    beta0 = norm1 / m[0]
    q = 1.0 + beta0
    alpha1 = norm1 / (q * q * m[1] - 2.0 * q * alpha0 * m[2] + alpha0 * alpha0 * m[3])
    r1, r2 = -(alpha0 + alpha1 * q), alpha0 * alpha1
    norm2 = (
        m[0]
        + 2.0 * r1 * m[1]
        + (r1 * r1 + 2.0 * r2) * m[2]
        + 2.0 * r1 * r2 * m[3]
        + r2 * r2 * m[4]
    )
    beta1 = norm2 / norm1
    d0, d1, d2 = 1.0 + beta1 * q, r1 - beta1 * alpha0, r2
    alpha2 = norm2 / (
        d0 * d0 * m[1]
        + 2.0 * d0 * d1 * m[2]
        + (d1 * d1 + 2.0 * d0 * d2) * m[3]
        + 2.0 * d1 * d2 * m[4]
        + d2 * d2 * m[5]
    )
    x0 = alpha0 + alpha1 * q + alpha2 * d0
    x1 = alpha2 * d1 - alpha1 * alpha0
    x2 = alpha2 * d2
    coefficients = [jnp.broadcast_to(v, (NODES, LANES)) for v in (x0, x1, x2)]
    for x in range(EX * NODES):
        for e in range(EY):
            rows = slice(8 * e, 8 * e + 8)
            v = [fields[k, x, rows, :] for k in range(ROUNDS)]
            solution_ref[x, rows, :] = (
                coefficients[0] * v[0] + coefficients[1] * v[1] + coefficients[2] * v[2]
            )
            residual_ref[x, rows, :] = v[0] - (
                coefficients[0] * v[1] + coefficients[1] * v[2] + coefficients[2] * v[3]
            )
    for copy in flight:
        copy.wait_send()
    whole(column, 0, in_column[0]).wait_send()
    whole(plane, 1, in_plane[0]).wait_send()


def solution(mesh):
    count_s, count_p = mesh.shape["stream"], mesh.shape["span"]

    def step(source, geometry):
        block = (EX * NODES, EY * NODES, LANES)
        anywhere = pl.BlockSpec(memory_space=pl.ANY)
        f32 = jnp.float32
        return pl.pallas_call(
            functools.partial(kernel, count_s, count_p),
            out_shape=[jax.ShapeDtypeStruct(block, f32)] * 2,
            in_specs=[anywhere] * 3,
            out_specs=[pl.BlockSpec(memory_space=pltpu.VMEM)] * 2,
            scratch_shapes=[
                pltpu.VMEM(block, f32),
                pltpu.VMEM((6,) + block, jnp.bfloat16),
                pltpu.VMEM((2 * LANES + 2 * NODES, LANES), f32),
                pltpu.VMEM((6,) + block, f32),
                pltpu.VMEM((ROUNDS,) + block, f32),
                pltpu.VMEM((ROUNDS,) + block, f32),
                pltpu.VMEM((ROUNDS, 2) + block[1:], f32),
                pltpu.VMEM((ROUNDS, 6, NODES, LANES), f32),
                pltpu.VMEM((ROUNDS, NODES, LANES), f32),
                pltpu.VMEM((EX * NODES * EY, NODES, LANES), f32),
                pltpu.VMEM(block, f32),
                pltpu.VMEM((1, LANES), f32),
                pltpu.VMEM((1, LANES), f32),
                pltpu.VMEM((Z * CORES - 1, LANES), f32),
                pltpu.VMEM((X * Y - 1, LANES), f32),
                pltpu.SemaphoreType.DMA((3,)),
                pltpu.SemaphoreType.DMA((ROUNDS, 8)),
                pltpu.SemaphoreType.DMA((ROUNDS, 8)),
                pltpu.SemaphoreType.DMA((2,)),
                pltpu.SemaphoreType.DMA((2,)),
            ],
            compiler_params=pltpu.CompilerParams(
                collective_id=0, has_side_effects=True, vmem_limit_bytes=48 * 1024 * 1024
            ),
        )(source, geometry, jnp.asarray(constants()))

    return jax.shard_map(
        step,
        mesh=mesh,
        in_specs=(P("stream", None, "span"), P(None, "stream", None, "span")),
        out_specs=(P("stream", None, "span"), P("stream", None, "span")),
        check_vma=False,
    )
```

```python
import functools

import jax
import jax.numpy as jnp
import numpy as np
from jax import lax
from jax.experimental import pallas as pl
from jax.experimental.pallas import tpu as pltpu
from jax.sharding import PartitionSpec as P

MESH = pl.DeviceIdType.MESH
NODES = 8
EX = 2
EY = 3
LANES = 128
ROUNDS = 4
ROWS = EX * NODES * EY * NODES
Z_HI, X, Y, CORES, Z_LO = 3, 4, 8, 2, 4
Z = Z_HI * Z_LO
HEADS = 2
FANOUT = (Z - HEADS) // HEADS


def gll_tables():
    points = np.array(
        [
            -1.0,
            -0.8717401485096066,
            -0.5917001814331423,
            -0.2092992179024789,
            0.2092992179024789,
            0.5917001814331423,
            0.8717401485096066,
            1.0,
        ]
    )
    weights = np.array(
        [
            1.0 / 28.0,
            0.2107042271435061,
            0.3411226924835044,
            0.4124587946587038,
            0.4124587946587038,
            0.3411226924835044,
            0.2107042271435061,
            1.0 / 28.0,
        ]
    )
    barycentric = np.array(
        [
            1.0 / np.prod([points[j] - points[k] for k in range(8) if k != j])
            for j in range(8)
        ]
    )
    derivative = np.zeros((8, 8))
    for j in range(8):
        for k in range(8):
            if j != k:
                derivative[j, k] = barycentric[k] / barycentric[j] / (points[j] - points[k])
    for j in range(8):
        derivative[j, j] = -np.sum(derivative[j])
    return weights, derivative


WEIGHTS, DERIVATIVE = gll_tables()


def constants():
    half = np.ones(NODES)
    half[0] = half[-1] = 0.5
    copies = LANES // NODES
    weight = WEIGHTS[:, None] * np.tile(WEIGHTS, copies)[None, :]
    halves = half[:, None] * np.tile(half, copies)[None, :]
    return np.concatenate([weight, halves]).astype(np.float32)


def matrices():
    blocks = np.kron(np.eye(LANES // NODES), DERIVATIVE).astype(np.float32)
    parts = []
    for matrix in (blocks, blocks.T):
        lead = matrix.astype(jnp.bfloat16)
        parts += [lead, (matrix - lead.astype(np.float32)).astype(jnp.bfloat16)]
    return np.stack(parts)


def split(values):
    lead = values.astype(jnp.bfloat16)
    return lead, (values - lead.astype(jnp.float32)).astype(jnp.bfloat16)


def along_z(parts, matrix):
    wide = jnp.concatenate([matrix[0], matrix[1]], axis=1)
    product = jnp.dot(
        jnp.concatenate(parts, axis=1),
        jnp.concatenate([wide, wide], axis=0),
        preferred_element_type=jnp.float32,
    )
    return product[:, :LANES] + product[:, LANES:]


def along_y(parts, matrix):
    tall = jnp.concatenate([matrix[0], matrix[1]], axis=0)
    stacked = [
        jnp.concatenate([part[LANES * r : LANES * r + LANES] for part in parts], axis=0)
        for r in range(ROWS // LANES)
    ]
    product = jnp.dot(
        jnp.concatenate([tall, tall], axis=1),
        jnp.concatenate(stacked, axis=1),
        preferred_element_type=jnp.float32,
    )
    product = product[:LANES] + product[LANES:]
    return [product[:, LANES * r : LANES * r + LANES] for r in range(ROWS // LANES)]


def neighbours(count_s, count_p):
    s, p = lax.axis_index("stream"), lax.axis_index("span")
    down, up = lax.rem(s + count_s - 1, count_s), lax.rem(s + 1, count_s)
    left, right = lax.rem(p + count_p - 1, count_p), lax.rem(p + 1, count_p)
    return s, p, down, up, left, right


def place(s, p):
    core, row = lax.rem(s, CORES), s // CORES
    y, x, z_hi = lax.rem(row, Y), lax.rem(row // Y, X), row // (X * Y)
    return core, x, y, z_hi * Z_LO + p, (x * Y + y) * CORES


def in_column(base, z, core):
    return base + (z // Z_LO) * (X * Y * CORES) + core, lax.rem(z, Z_LO)


def plane_peers(s, p):
    core, row = lax.rem(s, CORES), s // CORES
    y, x, z_hi = lax.rem(row, Y), lax.rem(row // Y, X), row // (X * Y)
    peers = []
    for dx in range(X):
        for dy in range(Y):
            if dx or dy:
                there = (z_hi * X + lax.rem(x + dx, X)) * Y + lax.rem(y + dy, Y)
                peers.append((there * CORES + core, p))
    return peers


def along_x(parts, matrix):
    even = [parts[j] + parts[7 - j] for j in range(4)]
    odd = [parts[j] - parts[7 - j] for j in range(4)]
    low, high = [None] * 4, [None] * 4
    for i in range(4):
        a = sum(odd[j] * float(0.5 * (matrix[i, j] - matrix[i, 7 - j])) for j in range(4))
        b = sum(even[j] * float(0.5 * (matrix[i, j] + matrix[i, 7 - j])) for j in range(4))
        low[i], high[i] = b + a, a - b
    return low + high[::-1]


def kernel(
    count_s,
    count_p,
    source_hbm,
    geometry_hbm,
    constant_hbm,
    matrix_hbm,
    solution_ref,
    residual_ref,
    source,
    geometry,
    constant,
    matrix,
    metric,
    fields,
    partial,
    planes,
    packs,
    packed,
    grad1,
    grad2,
    row1,
    row2,
    result,
    column,
    plane,
    load_sem,
    send_sem,
    recv_sem,
    sum_send,
    sum_recv,
):
    s, p, down, up, left, right = neighbours(count_s, count_p)
    core, _, _, z, base = place(s, p)
    gathers = z < HEADS
    halo = [(down, p), (up, p), (s, left), (s, right)]
    halo += [(down, left), (down, right), (up, left), (up, right)]
    in_plane = plane_peers(s, p)
    heads = [(h, c) for h in range(HEADS) for c in range(CORES)]
    below = [
        in_column(base, lax.rem(z + dz, Z), lax.rem(core + dc, CORES))
        for dz in range(Z)
        for dc in range(CORES)
        if dz or dc
    ]

    loads = [
        pltpu.make_async_copy(source_hbm, source, load_sem.at[0]),
        pltpu.make_async_copy(constant_hbm, constant, load_sem.at[1]),
        pltpu.make_async_copy(geometry_hbm, geometry, load_sem.at[2]),
        pltpu.make_async_copy(matrix_hbm, matrix, load_sem.at[3]),
    ]
    barrier = pltpu.get_barrier_semaphore()
    for peer in halo:
        pl.semaphore_signal(barrier, inc=1, device_id=peer, device_id_type=MESH)
    for load in loads:
        load.start()

    @pl.when(gathers)
    def _():
        for peer in in_plane + below:
            pl.semaphore_signal(barrier, inc=1, device_id=peer, device_id_type=MESH)


    lane = lax.broadcasted_iota(jnp.int32, (NODES, LANES), 1)
    sub = lax.broadcasted_iota(jnp.int32, (NODES, LANES), 0)
    node = lax.rem(lane, NODES)
    from_right = (node == NODES - 1) & (lane != LANES - 1)
    from_left = (node == 0) & (lane != 0)

    def assemble(values, k):
        tiles = [[values[x, 8 * e : 8 * e + 8] for e in range(EY)] for x in range(EX * NODES)]
        for e in range(EY):
            joined = tiles[NODES - 1][e] + tiles[NODES][e]
            tiles[NODES - 1][e] = tiles[NODES][e] = joined
        for x in range(EX * NODES):
            if x == NODES:
                for e in range(EY):
                    partial[k, x, 8 * e : 8 * e + 8, :] = tiles[NODES - 1][e]
                tiles[x] = tiles[NODES - 1]
                continue
            row = tiles[x]
            new = list(row)
            for e in range(EY - 1):
                new[e] = new[e] + jnp.where(sub == 7, pltpu.roll(row[e + 1], 7, 0), 0.0)
                new[e + 1] = new[e + 1] + jnp.where(sub == 0, pltpu.roll(row[e], 1, 0), 0.0)
            new[0] = jnp.where(sub == 0, 0.0, new[0])
            new[-1] = jnp.where(sub == 7, 0.0, new[-1])
            for e in range(EY):
                t = new[e]
                t = (
                    t
                    + jnp.where(from_right, pltpu.roll(t, LANES - 1, 1), 0.0)
                    + jnp.where(from_left, pltpu.roll(t, 1, 1), 0.0)
                )
                new[e] = t
                partial[k, x, 8 * e : 8 * e + 8, :] = t
            tiles[x] = new
        pack = jnp.zeros((NODES, LANES), jnp.float32)
        for x in range(EX * NODES):
            for e in range(EY):
                j = x * EY + e
                pack = jnp.where(lane // 2 == j, pltpu.roll(tiles[x][e], 2 * j + 1, 1), pack)
        packed[k] = pack

    last = EX * NODES - 1

    def exchanges(k):
        sources = [partial.at[k, 0], partial.at[k, last]] + [packed.at[k]] * 6
        targets = [planes.at[k, 1], planes.at[k, 0]]
        targets += [packs.at[k, i] for i in (1, 0, 5, 4, 3, 2)]
        slots = [1, 0, 3, 2, 7, 6, 5, 4]
        return [
            pltpu.make_async_remote_copy(
                src_ref=a,
                dst_ref=b,
                send_sem=send_sem.at[k, i],
                recv_sem=recv_sem.at[k, slots[i]],
                device_id=peer,
                device_id_type=MESH,
            )
            for i, (a, b, peer) in enumerate(zip(sources, targets, halo))
        ]

    def finish(k, want_norm):
        edge = EY * 2 * last
        low, high = lane < 2 * EY, (lane >= edge) & (lane < edge + 2 * EY)

        def with_corners(face, below, above):
            return (
                face
                + jnp.where(low, pltpu.roll(below, LANES - edge, 1), 0.0)
                + jnp.where(high, pltpu.roll(above, edge, 1), 0.0)
            )

        minus = with_corners(packs[k, 0], packs[k, 2], packs[k, 4])
        plus = with_corners(packs[k, 1], packs[k, 3], packs[k, 5])
        faces = jnp.where(
            lax.rem(lane, 2) == 0, pltpu.roll(plus, LANES - 1, 1), pltpu.roll(minus, 1, 1)
        )
        ends = (lane == 0) | (lane == LANES - 1)
        inner = jnp.zeros((NODES, LANES), jnp.float32)
        outer = jnp.zeros((NODES, LANES), jnp.float32)
        for x in range(EX * NODES):
            for e in range(EY):
                j = x * EY + e
                t = partial[k, x, 8 * e : 8 * e + 8, :]
                if x == 0:
                    t = t + planes[k, 0, 8 * e : 8 * e + 8, :]
                if x == last:
                    t = t + planes[k, 1, 8 * e : 8 * e + 8, :]
                t = t + jnp.where(ends, pltpu.roll(faces, LANES - 2 * j - 1, 1), 0.0)
                fields[k, x, 8 * e : 8 * e + 8, :] = t
                if want_norm:
                    if x % NODES in (0, NODES - 1):
                        outer = outer + t * t
                    else:
                        inner = inner + t * t
        return (inner + 0.5 * outer) * constant[NODES : 2 * NODES, :]

    def fluxes(k):
        values = fields[k]
        parts = split(values.reshape(ROWS, LANES))
        grad2[...] = along_z(parts, (matrix[2], matrix[3])).reshape(values.shape)
        for r, group in enumerate(along_y(parts, (matrix[0], matrix[1]))):
            grad1[16 * r : 16 * r + 16] = group.reshape(16, NODES, LANES)
        energy = jnp.zeros((NODES, LANES), jnp.float32)
        flux0 = {}
        for ex in range(EX):
            for e in range(EY):
                rows = slice(8 * e, 8 * e + 8)
                g0 = along_x([fields[k, ex * 8 + i, rows, :] for i in range(8)], DERIVATIVE)
                for i in range(8):
                    x = ex * 8 + i
                    j = x * EY + e
                    m = [metric[c, x, rows, :] for c in range(6)]
                    g1, g2 = grad1[j], grad2[x, rows, :]
                    f0 = m[0] * g0[i] + m[3] * g1 + m[4] * g2
                    f1 = m[3] * g0[i] + m[1] * g1 + m[5] * g2
                    f2 = m[4] * g0[i] + m[5] * g1 + m[2] * g2
                    energy = energy + (f0 * g0[i] + f1 * g1 + f2 * g2)
                    flux0[x, e] = f0
                    grad1[j] = f1
                    grad2[x, rows, :] = f2
        return flux0, energy

    def divergence(flux0):
        flat = split(grad2[...].reshape(ROWS, LANES))
        along2 = along_z(flat, (matrix[0], matrix[1])).reshape(EX * NODES, EY * NODES, LANES)
        flat = split(grad1[...].reshape(ROWS, LANES))
        for r, group in enumerate(along_y(flat, (matrix[2], matrix[3]))):
            grad1[16 * r : 16 * r + 16] = group.reshape(16, NODES, LANES)
        total = {}
        for ex in range(EX):
            for e in range(EY):
                back = along_x([flux0[ex * 8 + i, e] for i in range(8)], DERIVATIVE.T)
                for i in range(8):
                    x = ex * 8 + i
                    total[x, e] = (
                        back[i] + grad1[x * EY + e] + along2[x, 8 * e : 8 * e + 8]
                    )
        return jnp.stack(
            [
                jnp.concatenate([total[x, e] for e in range(EY)], axis=0)
                for x in range(EX * NODES)
            ]
        )

    def fold(tile, width):
        shift = LANES // 2
        while shift >= width:
            tile = tile + pltpu.roll(tile, shift, 1)
            shift //= 2
        return tile

    loads[0].wait()
    assemble(source[...], 0)
    pl.semaphore_wait(
        barrier,
        len(halo) + len(heads) + jnp.where(gathers, len(in_plane) - 1, 0),
    )
    flight = exchanges(0)
    for copy in flight:
        copy.start()
    loads[1].wait()
    loads[2].wait()
    loads[3].wait()
    weight = constant[0:NODES, :]
    for c in range(6):
        for x in range(EX * NODES):
            scaled = geometry[c, x].astype(jnp.float32)
            for e in range(EY):
                metric[c, x, 8 * e : 8 * e + 8, :] = scaled[8 * e : 8 * e + 8] * (
                    weight * float(WEIGHTS[x % NODES])
                )

    moments = []
    for k in range(ROUNDS - 1):
        for copy in flight:
            copy.wait_recv()
        moments.append(finish(k, True))
        flux0, energy = fluxes(k)
        moments.append(energy)
        if k == ROUNDS - 2:
            packed_moments = jnp.where(
                lane < 96, fold(moments[4], 32), fold(moments[5], 32)
            )
            for i in range(4):
                packed_moments = jnp.where(
                    lane // 16 == i, fold(moments[i], 16), packed_moments
                )
            row1[...] = jnp.sum(packed_moments, axis=0, keepdims=True)
            for head, c in heads:
                offset = lax.rem(z + Z - head, Z) * CORES + lax.rem(core + CORES - c, CORES)

                @pl.when(offset > 0)
                def _(head=head, c=c, offset=offset):
                    pltpu.make_async_remote_copy(
                        src_ref=row1,
                        dst_ref=column.at[offset - 1],
                        send_sem=sum_send.at[0],
                        recv_sem=sum_recv.at[0],
                        device_id=in_column(base, jnp.int32(head), c),
                        device_id_type=MESH,
                    ).start()

        for copy in flight:
            copy.wait_send()
        assemble(divergence(flux0), k + 1)
        flight = exchanges(k + 1)
        for copy in flight:
            copy.start()

    def whole(buffer, i):
        return pltpu.make_async_remote_copy(
            src_ref=buffer,
            dst_ref=buffer,
            send_sem=sum_send.at[i],
            recv_sem=sum_recv.at[i],
            device_id=halo[0],
            device_id_type=MESH,
        )

    @pl.when(gathers)
    def _():
        whole(column, 0).wait_recv()
        row2[...] = row1[...] + jnp.sum(column[...], axis=0)
        for i, peer in enumerate(in_plane):
            pltpu.make_async_remote_copy(
                src_ref=row2,
                dst_ref=plane.at[i],
                send_sem=sum_send.at[1],
                recv_sem=sum_recv.at[1],
                device_id=peer,
                device_id_type=MESH,
            ).start()

    for copy in flight:
        copy.wait_recv()
    finish(ROUNDS - 1, False)

    @pl.when(gathers)
    def _():
        whole(plane, 1).wait_recv()
        result[...] = row2[...] + jnp.sum(plane[...], axis=0)
        for i in range(FANOUT):
            target = jnp.where(z == 0, Z - 1 - i, HEADS + i)
            pltpu.make_async_remote_copy(
                src_ref=result,
                dst_ref=result,
                send_sem=sum_send.at[2],
                recv_sem=sum_recv.at[2],
                device_id=in_column(base, target, core),
                device_id_type=MESH,
            ).start()

    @pl.when(jnp.logical_not(gathers))
    def _():
        whole(result, 2).wait_recv()

    total = result[...]
    group = lax.broadcasted_iota(jnp.int32, (1, LANES), 1)
    bounds = [0, 16, 32, 48, 64, 96, 128]
    m = [
        jnp.sum(
            jnp.where((group >= bounds[i]) & (group < bounds[i + 1]), total, 0.0),
            axis=1,
            keepdims=True,
        )
        for i in range(6)
    ]
    alpha0 = m[0] / m[1]
    norm1 = alpha0 * alpha0 * m[2] - m[0]
    beta0 = norm1 / m[0]
    q = 1.0 + beta0
    alpha1 = norm1 / (q * q * m[1] - 2.0 * q * alpha0 * m[2] + alpha0 * alpha0 * m[3])
    r1, r2 = -(alpha0 + alpha1 * q), alpha0 * alpha1
    norm2 = (
        m[0]
        + 2.0 * r1 * m[1]
        + (r1 * r1 + 2.0 * r2) * m[2]
        + 2.0 * r1 * r2 * m[3]
        + r2 * r2 * m[4]
    )
    beta1 = norm2 / norm1
    d0, d1, d2 = 1.0 + beta1 * q, r1 - beta1 * alpha0, r2
    alpha2 = norm2 / (
        d0 * d0 * m[1]
        + 2.0 * d0 * d1 * m[2]
        + (d1 * d1 + 2.0 * d0 * d2) * m[3]
        + 2.0 * d1 * d2 * m[4]
        + d2 * d2 * m[5]
    )
    x0 = alpha0 + alpha1 * q + alpha2 * d0
    x1 = alpha2 * d1 - alpha1 * alpha0
    x2 = alpha2 * d2
    coefficients = [jnp.broadcast_to(v, (NODES, LANES)) for v in (x0, x1, x2)]
    for x in range(EX * NODES):
        for e in range(EY):
            rows = slice(8 * e, 8 * e + 8)
            v = [fields[k, x, rows, :] for k in range(ROUNDS)]
            solution_ref[x, rows, :] = (
                coefficients[0] * v[0] + coefficients[1] * v[1] + coefficients[2] * v[2]
            )
            residual_ref[x, rows, :] = v[0] - (
                coefficients[0] * v[1] + coefficients[1] * v[2] + coefficients[2] * v[3]
            )
    for copy in flight:
        copy.wait_send()

    @pl.when(gathers)
    def _():
        whole(column.at[pl.ds(0, len(heads) - 1)], 0).wait_send()
        whole(plane, 1).wait_send()
        whole(column.at[pl.ds(0, FANOUT)], 2).wait_send()

    @pl.when(jnp.logical_not(gathers))
    def _():
        whole(column.at[pl.ds(0, len(heads))], 0).wait_send()


def solution(mesh):
    count_s, count_p = mesh.shape["stream"], mesh.shape["span"]

    def step(source, geometry):
        block = (EX * NODES, EY * NODES, LANES)
        in_hbm = pl.BlockSpec(memory_space=pltpu.HBM)
        f32 = jnp.float32
        return pl.pallas_call(
            functools.partial(kernel, count_s, count_p),
            out_shape=[pltpu.VMEM(block, f32)] * 2,
            in_specs=[in_hbm] * 4,
            out_specs=[pl.BlockSpec(memory_space=pltpu.VMEM)] * 2,
            scratch_shapes=[
                pltpu.VMEM(block, f32),
                pltpu.VMEM((6,) + block, jnp.bfloat16),
                pltpu.VMEM((2 * NODES, LANES), f32),
                pltpu.VMEM((4, LANES, LANES), jnp.bfloat16),
                pltpu.VMEM((6,) + block, f32),
                pltpu.VMEM((ROUNDS,) + block, f32),
                pltpu.VMEM((ROUNDS,) + block, f32),
                pltpu.VMEM((ROUNDS, 2) + block[1:], f32),
                pltpu.VMEM((ROUNDS, 6, NODES, LANES), f32),
                pltpu.VMEM((ROUNDS, NODES, LANES), f32),
                pltpu.VMEM((EX * NODES * EY, NODES, LANES), f32),
                pltpu.VMEM(block, f32),
                pltpu.VMEM((1, LANES), f32),
                pltpu.VMEM((1, LANES), f32),
                pltpu.VMEM((1, LANES), f32),
                pltpu.VMEM((Z * CORES - 1, 1, LANES), f32),
                pltpu.VMEM((X * Y - 1, 1, LANES), f32),
                pltpu.SemaphoreType.DMA((4,)),
                pltpu.SemaphoreType.DMA((ROUNDS, 8)),
                pltpu.SemaphoreType.DMA((ROUNDS, 8)),
                pltpu.SemaphoreType.DMA((3,)),
                pltpu.SemaphoreType.DMA((3,)),
            ],
            compiler_params=pltpu.CompilerParams(
                collective_id=0, has_side_effects=True, vmem_limit_bytes=48 * 1024 * 1024
            ),
        )(*(pltpu.with_memory_space_constraint(v, pltpu.HBM) for v in (source, geometry, jnp.asarray(constants()), jnp.asarray(matrices()))))

    return jax.shard_map(
        step,
        mesh=mesh,
        in_specs=(P("stream", None, "span"), P(None, "stream", None, "span")),
        out_specs=(P("stream", None, "span"), P("stream", None, "span")),
        check_vma=False,
    )
```

```python
import functools

import jax
import jax.numpy as jnp
import numpy as np
from jax import lax
from jax.experimental import pallas as pl
from jax.experimental.pallas import tpu as pltpu
from jax.sharding import PartitionSpec as P

MESH = pl.DeviceIdType.MESH
NODES = 8
EX = 2
EY = 3
LANES = 128
ROUNDS = 4
ROWS = EX * NODES * EY * NODES
Z_HI, X, Y, CORES, Z_LO = 3, 4, 8, 2, 4
Z = Z_HI * Z_LO
HEADS = 2
FANOUT = (Z - HEADS) // HEADS


def gll_tables():
    points = np.array(
        [
            -1.0,
            -0.8717401485096066,
            -0.5917001814331423,
            -0.2092992179024789,
            0.2092992179024789,
            0.5917001814331423,
            0.8717401485096066,
            1.0,
        ]
    )
    weights = np.array(
        [
            1.0 / 28.0,
            0.2107042271435061,
            0.3411226924835044,
            0.4124587946587038,
            0.4124587946587038,
            0.3411226924835044,
            0.2107042271435061,
            1.0 / 28.0,
        ]
    )
    barycentric = np.array(
        [
            1.0 / np.prod([points[j] - points[k] for k in range(8) if k != j])
            for j in range(8)
        ]
    )
    derivative = np.zeros((8, 8))
    for j in range(8):
        for k in range(8):
            if j != k:
                derivative[j, k] = barycentric[k] / barycentric[j] / (points[j] - points[k])
    for j in range(8):
        derivative[j, j] = -np.sum(derivative[j])
    return weights, derivative


WEIGHTS, DERIVATIVE = gll_tables()


def constants():
    half = np.ones(NODES)
    half[0] = half[-1] = 0.5
    copies = LANES // NODES
    weight = WEIGHTS[:, None] * np.tile(WEIGHTS, copies)[None, :]
    halves = half[:, None] * np.tile(half, copies)[None, :]
    return np.concatenate([weight, halves]).astype(np.float32)


def matrices():
    blocks = np.kron(np.eye(LANES // NODES), DERIVATIVE).astype(np.float32)
    parts = []
    for matrix in (blocks, blocks.T):
        lead = matrix.astype(jnp.bfloat16)
        parts += [lead, (matrix - lead.astype(np.float32)).astype(jnp.bfloat16)]
    return np.stack(parts)


def split(values):
    lead = values.astype(jnp.bfloat16)
    return lead, (values - lead.astype(jnp.float32)).astype(jnp.bfloat16)


def along_z(parts, matrix):
    wide = jnp.concatenate([matrix[0], matrix[1]], axis=1)
    product = jnp.dot(
        jnp.concatenate(parts, axis=1),
        jnp.concatenate([wide, wide], axis=0),
        preferred_element_type=jnp.float32,
    )
    return product[:, :LANES] + product[:, LANES:]


def along_y(parts, matrix):
    groups = parts[0].shape[0] // LANES
    tall = jnp.concatenate([matrix[0], matrix[1]], axis=0)
    stacked = [
        jnp.concatenate([part[LANES * r : LANES * r + LANES] for part in parts], axis=0)
        for r in range(groups)
    ]
    product = jnp.dot(
        jnp.concatenate([tall, tall], axis=1),
        jnp.concatenate(stacked, axis=1),
        preferred_element_type=jnp.float32,
    )
    product = product[:LANES] + product[LANES:]
    return [product[:, LANES * r : LANES * r + LANES] for r in range(groups)]


def neighbours(count_s, count_p):
    s, p = lax.axis_index("stream"), lax.axis_index("span")
    down, up = lax.rem(s + count_s - 1, count_s), lax.rem(s + 1, count_s)
    left, right = lax.rem(p + count_p - 1, count_p), lax.rem(p + 1, count_p)
    return s, p, down, up, left, right


def place(s, p):
    core, row = lax.rem(s, CORES), s // CORES
    y, x, z_hi = lax.rem(row, Y), lax.rem(row // Y, X), row // (X * Y)
    return core, x, y, z_hi * Z_LO + p, (x * Y + y) * CORES


def in_column(base, z, core):
    return base + (z // Z_LO) * (X * Y * CORES) + core, lax.rem(z, Z_LO)


def plane_peers(s, p):
    core, row = lax.rem(s, CORES), s // CORES
    y, x, z_hi = lax.rem(row, Y), lax.rem(row // Y, X), row // (X * Y)
    peers = []
    for dx in range(X):
        for dy in range(Y):
            if dx or dy:
                there = (z_hi * X + lax.rem(x + dx, X)) * Y + lax.rem(y + dy, Y)
                peers.append((there * CORES + core, p))
    return peers


def along_x(parts, matrix):
    even = [parts[j] + parts[7 - j] for j in range(4)]
    odd = [parts[j] - parts[7 - j] for j in range(4)]
    low, high = [None] * 4, [None] * 4
    for i in range(4):
        a = sum(odd[j] * float(0.5 * (matrix[i, j] - matrix[i, 7 - j])) for j in range(4))
        b = sum(even[j] * float(0.5 * (matrix[i, j] + matrix[i, 7 - j])) for j in range(4))
        low[i], high[i] = b + a, a - b
    return low + high[::-1]


def kernel(
    count_s,
    count_p,
    source_hbm,
    geometry_hbm,
    constant_hbm,
    matrix_hbm,
    solution_ref,
    residual_ref,
    source,
    geometry,
    constant,
    matrix,
    metric,
    fields,
    partial,
    planes,
    packs,
    packed,
    early,
    early_pack,
    own_side,
    far_side,
    face,
    response,
    grad1,
    grad2,
    row1,
    row2,
    result,
    column,
    plane,
    load_sem,
    send_sem,
    recv_sem,
    sum_send,
    sum_recv,
    side_sem,
):
    s, p, down, up, left, right = neighbours(count_s, count_p)
    core, _, _, z, base = place(s, p)
    gathers = z < HEADS
    block = X * Y * CORES
    long_down = lax.rem(s, block) == 0
    long_up = lax.rem(s, block) == block - 1
    is_long = long_down | long_up
    halo = [(down, p), (up, p), (s, left), (s, right)]
    halo += [(down, left), (down, right), (up, left), (up, right)]
    in_plane = plane_peers(s, p)
    heads = [(h, c) for h in range(HEADS) for c in range(CORES)]
    below = [
        in_column(base, lax.rem(z + dz, Z), lax.rem(core + dc, CORES))
        for dz in range(Z)
        for dc in range(CORES)
        if dz or dc
    ]

    loads = [
        pltpu.make_async_copy(source_hbm, source, load_sem.at[0]),
        pltpu.make_async_copy(constant_hbm, constant, load_sem.at[1]),
        pltpu.make_async_copy(geometry_hbm, geometry, load_sem.at[2]),
        pltpu.make_async_copy(matrix_hbm, matrix, load_sem.at[3]),
    ]
    barrier = pltpu.get_barrier_semaphore()
    for peer in halo:
        pl.semaphore_signal(barrier, inc=1, device_id=peer, device_id_type=MESH)
    for load in loads:
        load.start()

    @pl.when(gathers)
    def _():
        for peer in in_plane + below:
            pl.semaphore_signal(barrier, inc=1, device_id=peer, device_id_type=MESH)


    lane = lax.broadcasted_iota(jnp.int32, (NODES, LANES), 1)
    sub = lax.broadcasted_iota(jnp.int32, (NODES, LANES), 0)
    node = lax.rem(lane, NODES)
    from_right = (node == NODES - 1) & (lane != LANES - 1)
    from_left = (node == 0) & (lane != 0)

    def assemble(values, sums, pack_ref):
        tiles = [[values[x, 8 * e : 8 * e + 8] for e in range(EY)] for x in range(EX * NODES)]
        for e in range(EY):
            joined = tiles[NODES - 1][e] + tiles[NODES][e]
            tiles[NODES - 1][e] = tiles[NODES][e] = joined
        for x in range(EX * NODES):
            if x == NODES:
                for e in range(EY):
                    sums[x, 8 * e : 8 * e + 8, :] = tiles[NODES - 1][e]
                tiles[x] = tiles[NODES - 1]
                continue
            row = tiles[x]
            new = list(row)
            for e in range(EY - 1):
                new[e] = new[e] + jnp.where(sub == 7, pltpu.roll(row[e + 1], 7, 0), 0.0)
                new[e + 1] = new[e + 1] + jnp.where(sub == 0, pltpu.roll(row[e], 1, 0), 0.0)
            new[0] = jnp.where(sub == 0, 0.0, new[0])
            new[-1] = jnp.where(sub == 7, 0.0, new[-1])
            for e in range(EY):
                t = new[e]
                t = (
                    t
                    + jnp.where(from_right, pltpu.roll(t, LANES - 1, 1), 0.0)
                    + jnp.where(from_left, pltpu.roll(t, 1, 1), 0.0)
                )
                new[e] = t
                sums[x, 8 * e : 8 * e + 8, :] = t
            tiles[x] = new
        pack = jnp.zeros((NODES, LANES), jnp.float32)
        for x in range(EX * NODES):
            for e in range(EY):
                j = x * EY + e
                pack = jnp.where(lane // 2 == j, pltpu.roll(tiles[x][e], 2 * j + 1, 1), pack)
        pack_ref[...] = pack

    last = EX * NODES - 1

    def exchanges(k, sums=None, pack_ref=None):
        sums = partial.at[k] if sums is None else sums
        pack_ref = packed.at[k] if pack_ref is None else pack_ref
        sources = [sums.at[0], sums.at[last]] + [pack_ref] * 6
        targets = [planes.at[k, 1], planes.at[k, 0]]
        targets += [packs.at[k, i] for i in (1, 0, 5, 4, 3, 2)]
        slots = [1, 0, 3, 2, 7, 6, 5, 4]
        return [
            pltpu.make_async_remote_copy(
                src_ref=a,
                dst_ref=b,
                send_sem=send_sem.at[k, i],
                recv_sem=recv_sem.at[k, slots[i]],
                device_id=peer,
                device_id_type=MESH,
            )
            for i, (a, b, peer) in enumerate(zip(sources, targets, halo))
        ]

    def finish(k, want_norm, with_down=True, with_up=True):
        edge = EY * 2 * last
        low, high = lane < 2 * EY, (lane >= edge) & (lane < edge + 2 * EY)

        def with_corners(face, below, above):
            if with_down:
                face = face + jnp.where(low, pltpu.roll(packs[k, below], LANES - edge, 1), 0.0)
            if with_up:
                face = face + jnp.where(high, pltpu.roll(packs[k, above], edge, 1), 0.0)
            return face

        minus = with_corners(packs[k, 0], 2, 4)
        plus = with_corners(packs[k, 1], 3, 5)
        faces = jnp.where(
            lax.rem(lane, 2) == 0, pltpu.roll(plus, LANES - 1, 1), pltpu.roll(minus, 1, 1)
        )
        ends = (lane == 0) | (lane == LANES - 1)
        inner = jnp.zeros((NODES, LANES), jnp.float32)
        outer = jnp.zeros((NODES, LANES), jnp.float32)
        for x in range(EX * NODES):
            for e in range(EY):
                j = x * EY + e
                t = partial[k, x, 8 * e : 8 * e + 8, :]
                if x == 0 and with_down:
                    t = t + planes[k, 0, 8 * e : 8 * e + 8, :]
                if x == last and with_up:
                    t = t + planes[k, 1, 8 * e : 8 * e + 8, :]
                t = t + jnp.where(ends, pltpu.roll(faces, LANES - 2 * j - 1, 1), 0.0)
                fields[k, x, 8 * e : 8 * e + 8, :] = t
                if want_norm:
                    if x % NODES in (0, NODES - 1):
                        outer = outer + t * t
                    else:
                        inner = inner + t * t
        return (inner + 0.5 * outer) * constant[NODES : 2 * NODES, :]

    def fluxes(k):
        values = fields[k]
        parts = split(values.reshape(ROWS, LANES))
        grad2[...] = along_z(parts, (matrix[2], matrix[3])).reshape(values.shape)
        for r, group in enumerate(along_y(parts, (matrix[0], matrix[1]))):
            grad1[16 * r : 16 * r + 16] = group.reshape(16, NODES, LANES)
        energy = jnp.zeros((NODES, LANES), jnp.float32)
        flux0 = {}
        for ex in range(EX):
            for e in range(EY):
                rows = slice(8 * e, 8 * e + 8)
                g0 = along_x([fields[k, ex * 8 + i, rows, :] for i in range(8)], DERIVATIVE)
                for i in range(8):
                    x = ex * 8 + i
                    j = x * EY + e
                    m = [metric[c, x, rows, :] for c in range(6)]
                    g1, g2 = grad1[j], grad2[x, rows, :]
                    f0 = m[0] * g0[i] + m[3] * g1 + m[4] * g2
                    f1 = m[3] * g0[i] + m[1] * g1 + m[5] * g2
                    f2 = m[4] * g0[i] + m[5] * g1 + m[2] * g2
                    energy = energy + (f0 * g0[i] + f1 * g1 + f2 * g2)
                    flux0[x, e] = f0
                    grad1[j] = f1
                    grad2[x, rows, :] = f2
        return flux0, energy

    def divergence(flux0, add=False):
        flat = split(grad2[...].reshape(ROWS, LANES))
        along2 = along_z(flat, (matrix[0], matrix[1])).reshape(EX * NODES, EY * NODES, LANES)
        flat = split(grad1[...].reshape(ROWS, LANES))
        for r, group in enumerate(along_y(flat, (matrix[2], matrix[3]))):
            grad1[16 * r : 16 * r + 16] = group.reshape(16, NODES, LANES)
        total = {}
        for ex in range(EX):
            for e in range(EY):
                back = along_x([flux0[ex * 8 + i, e] for i in range(8)], DERIVATIVE.T)
                for i in range(8):
                    x = ex * 8 + i
                    total[x, e] = (
                        back[i] + grad1[x * EY + e] + along2[x, 8 * e : 8 * e + 8]
                    )
        if add:
            for e in range(EY):
                extra = response[8 * e : 8 * e + 8, :]
                total[0, e] = total[0, e] + jnp.where(long_down, extra, 0.0)
                total[last, e] = total[last, e] + jnp.where(long_up, extra, 0.0)
        return jnp.stack(
            [
                jnp.concatenate([total[x, e] for e in range(EY)], axis=0)
                for x in range(EX * NODES)
            ]
        )

    def side_copy():
        return pltpu.make_async_remote_copy(
            src_ref=own_side,
            dst_ref=far_side,
            send_sem=side_sem.at[0],
            recv_sem=side_sem.at[1],
            device_id=(jnp.where(long_down, down, up), p),
            device_id_type=MESH,
        )

    def describe_side(first, plane_index):
        squares = DERIVATIVE[:, 0 if first == 0 else NODES - 1] ** 2
        own_side[0] = sum(metric[0, first + i] * float(squares[i]) for i in range(NODES))
        for c in range(1, 6):
            own_side[c] = metric[c, plane_index]

    def respond():
        values = face[...]
        rest = jnp.zeros((LANES - EY * NODES, LANES), jnp.float32)
        slope = jnp.where(
            long_down, float(DERIVATIVE[NODES - 1, NODES - 1]), float(DERIVATIVE[0, 0])
        )

        def tall(v):
            return split(jnp.concatenate([v, rest], axis=0))

        parts = tall(values)
        d1 = along_y(parts, (matrix[0], matrix[1]))[0][: EY * NODES]
        d2 = along_z(parts, (matrix[2], matrix[3]))[: EY * NODES]
        d0 = slope * values
        f1 = far_side[3] * d0 + far_side[1] * d1 + far_side[5] * d2
        f2 = far_side[4] * d0 + far_side[5] * d1 + far_side[2] * d2
        response[...] = (
            far_side[0] * values
            + slope * (far_side[3] * d1 + far_side[4] * d2)
            + along_y(tall(f1), (matrix[2], matrix[3]))[0][: EY * NODES]
            + along_z(tall(f2), (matrix[0], matrix[1]))[: EY * NODES]
        )

    def fold(tile, width):
        shift = LANES // 2
        while shift >= width:
            tile = tile + pltpu.roll(tile, shift, 1)
            shift //= 2
        return tile

    loads[0].wait()
    assemble(source[...], partial.at[0], packed.at[0])
    pl.semaphore_wait(
        barrier,
        len(halo) + len(heads) + jnp.where(gathers, len(in_plane) - 1, 0),
    )
    flight = exchanges(0)
    for copy in flight:
        copy.start()
    loads[1].wait()
    loads[2].wait()
    loads[3].wait()
    weight = constant[0:NODES, :]
    for c in range(6):
        for x in range(EX * NODES):
            scaled = geometry[c, x].astype(jnp.float32)
            for e in range(EY):
                metric[c, x, 8 * e : 8 * e + 8, :] = scaled[8 * e : 8 * e + 8] * (
                    weight * float(WEIGHTS[x % NODES])
                )

    to_down, to_up = (0, 4, 5), (1, 6, 7)
    from_down, from_up = to_up, to_down

    def ahead(copies_from, copies_to, side_first, side_plane, **skip):
        describe_side(side_first, side_plane)
        side_copy().start()
        for i, copy in enumerate(flight):
            if i not in copies_from:
                copy.wait_recv()
        finish(0, False, **skip)
        face[...] = fields[0, side_plane]
        flux, _ = fluxes(0)
        assemble(divergence(flux), early, early_pack)
        for i, copy in enumerate(exchanges(1, early, early_pack)):
            if i in copies_to:
                copy.start()
        for i, copy in enumerate(flight):
            if i in copies_from:
                copy.wait_recv()

    @pl.when(long_down)
    def _():
        ahead(from_down, to_down, 0, 0, with_down=False)

    @pl.when(long_up)
    def _():
        ahead(from_up, to_up, NODES, last, with_up=False)

    @pl.when(jnp.logical_not(is_long))
    def _():
        for copy in flight:
            copy.wait_recv()

    moments = []
    for k in range(ROUNDS - 1):
        if k > 0:
            for copy in flight:
                copy.wait_recv()
        moments.append(finish(k, True))
        flux0, energy = fluxes(k)
        moments.append(energy)
        if k == ROUNDS - 2:
            packed_moments = jnp.where(
                lane < 96, fold(moments[4], 32), fold(moments[5], 32)
            )
            for i in range(4):
                packed_moments = jnp.where(
                    lane // 16 == i, fold(moments[i], 16), packed_moments
                )
            row1[...] = jnp.sum(packed_moments, axis=0, keepdims=True)
            for head, c in heads:
                offset = lax.rem(z + Z - head, Z) * CORES + lax.rem(core + CORES - c, CORES)

                @pl.when(offset > 0)
                def _(head=head, c=c, offset=offset):
                    pltpu.make_async_remote_copy(
                        src_ref=row1,
                        dst_ref=column.at[offset - 1],
                        send_sem=sum_send.at[0],
                        recv_sem=sum_recv.at[0],
                        device_id=in_column(base, jnp.int32(head), c),
                        device_id_type=MESH,
                    ).start()

        for copy in flight:
            copy.wait_send()
        if k == 0:

            @pl.when(is_long)
            def _():
                side_copy().wait_recv()
                respond()

        assemble(divergence(flux0, k == 0), partial.at[k + 1], packed.at[k + 1])
        flight = exchanges(k + 1)
        for i, copy in enumerate(flight):
            if k > 0 or i in (2, 3):
                copy.start()
            else:
                pl.when(jnp.logical_not(long_down if i in to_down else long_up))(copy.start)

    def whole(buffer, i):
        return pltpu.make_async_remote_copy(
            src_ref=buffer,
            dst_ref=buffer,
            send_sem=sum_send.at[i],
            recv_sem=sum_recv.at[i],
            device_id=halo[0],
            device_id_type=MESH,
        )

    @pl.when(gathers)
    def _():
        whole(column, 0).wait_recv()
        row2[...] = row1[...] + jnp.sum(column[...], axis=0)
        for i, peer in enumerate(in_plane):
            pltpu.make_async_remote_copy(
                src_ref=row2,
                dst_ref=plane.at[i],
                send_sem=sum_send.at[1],
                recv_sem=sum_recv.at[1],
                device_id=peer,
                device_id_type=MESH,
            ).start()

    for copy in flight:
        copy.wait_recv()
    finish(ROUNDS - 1, False)

    @pl.when(gathers)
    def _():
        whole(plane, 1).wait_recv()
        result[...] = row2[...] + jnp.sum(plane[...], axis=0)
        for i in range(FANOUT):
            target = jnp.where(z == 0, Z - 1 - i, HEADS + i)
            pltpu.make_async_remote_copy(
                src_ref=result,
                dst_ref=result,
                send_sem=sum_send.at[2],
                recv_sem=sum_recv.at[2],
                device_id=in_column(base, target, core),
                device_id_type=MESH,
            ).start()

    @pl.when(jnp.logical_not(gathers))
    def _():
        whole(result, 2).wait_recv()

    total = result[...]
    group = lax.broadcasted_iota(jnp.int32, (1, LANES), 1)
    bounds = [0, 16, 32, 48, 64, 96, 128]
    m = [
        jnp.sum(
            jnp.where((group >= bounds[i]) & (group < bounds[i + 1]), total, 0.0),
            axis=1,
            keepdims=True,
        )
        for i in range(6)
    ]
    alpha0 = m[0] / m[1]
    norm1 = alpha0 * alpha0 * m[2] - m[0]
    beta0 = norm1 / m[0]
    q = 1.0 + beta0
    alpha1 = norm1 / (q * q * m[1] - 2.0 * q * alpha0 * m[2] + alpha0 * alpha0 * m[3])
    r1, r2 = -(alpha0 + alpha1 * q), alpha0 * alpha1
    norm2 = (
        m[0]
        + 2.0 * r1 * m[1]
        + (r1 * r1 + 2.0 * r2) * m[2]
        + 2.0 * r1 * r2 * m[3]
        + r2 * r2 * m[4]
    )
    beta1 = norm2 / norm1
    d0, d1, d2 = 1.0 + beta1 * q, r1 - beta1 * alpha0, r2
    alpha2 = norm2 / (
        d0 * d0 * m[1]
        + 2.0 * d0 * d1 * m[2]
        + (d1 * d1 + 2.0 * d0 * d2) * m[3]
        + 2.0 * d1 * d2 * m[4]
        + d2 * d2 * m[5]
    )
    x0 = alpha0 + alpha1 * q + alpha2 * d0
    x1 = alpha2 * d1 - alpha1 * alpha0
    x2 = alpha2 * d2
    coefficients = [jnp.broadcast_to(v, (NODES, LANES)) for v in (x0, x1, x2)]
    for x in range(EX * NODES):
        for e in range(EY):
            rows = slice(8 * e, 8 * e + 8)
            v = [fields[k, x, rows, :] for k in range(ROUNDS)]
            solution_ref[x, rows, :] = (
                coefficients[0] * v[0] + coefficients[1] * v[1] + coefficients[2] * v[2]
            )
            residual_ref[x, rows, :] = v[0] - (
                coefficients[0] * v[1] + coefficients[1] * v[2] + coefficients[2] * v[3]
            )
    for copy in flight:
        copy.wait_send()

    @pl.when(is_long)
    def _():
        side_copy().wait_send()

    @pl.when(gathers)
    def _():
        whole(column.at[pl.ds(0, len(heads) - 1)], 0).wait_send()
        whole(plane, 1).wait_send()
        whole(column.at[pl.ds(0, FANOUT)], 2).wait_send()

    @pl.when(jnp.logical_not(gathers))
    def _():
        whole(column.at[pl.ds(0, len(heads))], 0).wait_send()


def solution(mesh):
    count_s, count_p = mesh.shape["stream"], mesh.shape["span"]

    def step(source, geometry):
        block = (EX * NODES, EY * NODES, LANES)
        in_hbm = pl.BlockSpec(memory_space=pltpu.HBM)
        f32 = jnp.float32
        return pl.pallas_call(
            functools.partial(kernel, count_s, count_p),
            out_shape=[pltpu.VMEM(block, f32)] * 2,
            in_specs=[in_hbm] * 4,
            out_specs=[pl.BlockSpec(memory_space=pltpu.VMEM)] * 2,
            scratch_shapes=[
                pltpu.VMEM(block, f32),
                pltpu.VMEM((6,) + block, jnp.bfloat16),
                pltpu.VMEM((2 * NODES, LANES), f32),
                pltpu.VMEM((4, LANES, LANES), jnp.bfloat16),
                pltpu.VMEM((6,) + block, f32),
                pltpu.VMEM((ROUNDS,) + block, f32),
                pltpu.VMEM((ROUNDS,) + block, f32),
                pltpu.VMEM((ROUNDS, 2) + block[1:], f32),
                pltpu.VMEM((ROUNDS, 6, NODES, LANES), f32),
                pltpu.VMEM((ROUNDS, NODES, LANES), f32),
                pltpu.VMEM(block, f32),
                pltpu.VMEM((NODES, LANES), f32),
                pltpu.VMEM((6,) + block[1:], f32),
                pltpu.VMEM((6,) + block[1:], f32),
                pltpu.VMEM(block[1:], f32),
                pltpu.VMEM(block[1:], f32),
                pltpu.VMEM((EX * NODES * EY, NODES, LANES), f32),
                pltpu.VMEM(block, f32),
                pltpu.VMEM((1, LANES), f32),
                pltpu.VMEM((1, LANES), f32),
                pltpu.VMEM((1, LANES), f32),
                pltpu.VMEM((Z * CORES - 1, 1, LANES), f32),
                pltpu.VMEM((X * Y - 1, 1, LANES), f32),
                pltpu.SemaphoreType.DMA((4,)),
                pltpu.SemaphoreType.DMA((ROUNDS, 8)),
                pltpu.SemaphoreType.DMA((ROUNDS, 8)),
                pltpu.SemaphoreType.DMA((3,)),
                pltpu.SemaphoreType.DMA((3,)),
                pltpu.SemaphoreType.DMA((2,)),
            ],
            compiler_params=pltpu.CompilerParams(
                collective_id=0, has_side_effects=True, vmem_limit_bytes=48 * 1024 * 1024
            ),
        )(*(pltpu.with_memory_space_constraint(v, pltpu.HBM) for v in (source, geometry, jnp.asarray(constants()), jnp.asarray(matrices()))))

    return jax.shard_map(
        step,
        mesh=mesh,
        in_specs=(P("stream", None, "span"), P(None, "stream", None, "span")),
        out_specs=(P("stream", None, "span"), P("stream", None, "span")),
        check_vma=False,
    )
```

```python
import functools

import jax
import jax.numpy as jnp
import numpy as np
from jax import lax
from jax.experimental import pallas as pl
from jax.experimental.pallas import tpu as pltpu
from jax.sharding import PartitionSpec as P

MESH = pl.DeviceIdType.MESH
NODES = 8
EX = 2
EY = 3
LANES = 128
ROUNDS = 4
ROWS = EX * NODES * EY * NODES
Z_HI, X, Y, CORES, Z_LO = 3, 4, 8, 2, 4
Z = Z_HI * Z_LO
HEADS = 2
FANOUT = (Z - HEADS) // HEADS


def gll_tables():
    points = np.array(
        [
            -1.0,
            -0.8717401485096066,
            -0.5917001814331423,
            -0.2092992179024789,
            0.2092992179024789,
            0.5917001814331423,
            0.8717401485096066,
            1.0,
        ]
    )
    weights = np.array(
        [
            1.0 / 28.0,
            0.2107042271435061,
            0.3411226924835044,
            0.4124587946587038,
            0.4124587946587038,
            0.3411226924835044,
            0.2107042271435061,
            1.0 / 28.0,
        ]
    )
    barycentric = np.array(
        [
            1.0 / np.prod([points[j] - points[k] for k in range(8) if k != j])
            for j in range(8)
        ]
    )
    derivative = np.zeros((8, 8))
    for j in range(8):
        for k in range(8):
            if j != k:
                derivative[j, k] = barycentric[k] / barycentric[j] / (points[j] - points[k])
    for j in range(8):
        derivative[j, j] = -np.sum(derivative[j])
    return weights, derivative


WEIGHTS, DERIVATIVE = gll_tables()


def constants():
    half = np.ones(NODES)
    half[0] = half[-1] = 0.5
    copies = LANES // NODES
    weight = WEIGHTS[:, None] * np.tile(WEIGHTS, copies)[None, :]
    halves = half[:, None] * np.tile(half, copies)[None, :]
    return np.concatenate([weight, halves]).astype(np.float32)


def matrices():
    blocks = np.kron(np.eye(LANES // NODES), DERIVATIVE).astype(np.float32)
    parts = []
    for matrix in (blocks, blocks.T):
        lead = matrix.astype(jnp.bfloat16)
        parts += [lead, (matrix - lead.astype(np.float32)).astype(jnp.bfloat16)]
    return np.stack(parts)


def split(values):
    lead = values.astype(jnp.bfloat16)
    return lead, (values - lead.astype(jnp.float32)).astype(jnp.bfloat16)


def along_z(parts, matrix):
    wide = jnp.concatenate([matrix[0], matrix[1]], axis=1)
    product = jnp.dot(
        jnp.concatenate(parts, axis=1),
        jnp.concatenate([wide, wide], axis=0),
        preferred_element_type=jnp.float32,
    )
    return product[:, :LANES] + product[:, LANES:]


def along_y(parts, matrix):
    groups = parts[0].shape[0] // LANES
    tall = jnp.concatenate([matrix[0], matrix[1]], axis=0)
    stacked = [
        jnp.concatenate([part[LANES * r : LANES * r + LANES] for part in parts], axis=0)
        for r in range(groups)
    ]
    product = jnp.dot(
        jnp.concatenate([tall, tall], axis=1),
        jnp.concatenate(stacked, axis=1),
        preferred_element_type=jnp.float32,
    )
    product = product[:LANES] + product[LANES:]
    return [product[:, LANES * r : LANES * r + LANES] for r in range(groups)]


def neighbours(count_s, count_p):
    s, p = lax.axis_index("stream"), lax.axis_index("span")
    down, up = lax.rem(s + count_s - 1, count_s), lax.rem(s + 1, count_s)
    left, right = lax.rem(p + count_p - 1, count_p), lax.rem(p + 1, count_p)
    return s, p, down, up, left, right


def place(s, p):
    core, row = lax.rem(s, CORES), s // CORES
    y, x, z_hi = lax.rem(row, Y), lax.rem(row // Y, X), row // (X * Y)
    return core, x, y, z_hi * Z_LO + p, (x * Y + y) * CORES


def in_column(base, z, core):
    return base + (z // Z_LO) * (X * Y * CORES) + core, lax.rem(z, Z_LO)


def plane_peers(s, p):
    core, row = lax.rem(s, CORES), s // CORES
    y, x, z_hi = lax.rem(row, Y), lax.rem(row // Y, X), row // (X * Y)
    peers = []
    for dx in range(X):
        for dy in range(Y):
            if dx or dy:
                there = (z_hi * X + lax.rem(x + dx, X)) * Y + lax.rem(y + dy, Y)
                peers.append((there * CORES + core, p))
    return peers


def along_x(parts, matrix):
    even = [parts[j] + parts[7 - j] for j in range(4)]
    odd = [parts[j] - parts[7 - j] for j in range(4)]
    low, high = [None] * 4, [None] * 4
    for i in range(4):
        a = sum(odd[j] * float(0.5 * (matrix[i, j] - matrix[i, 7 - j])) for j in range(4))
        b = sum(even[j] * float(0.5 * (matrix[i, j] + matrix[i, 7 - j])) for j in range(4))
        low[i], high[i] = b + a, a - b
    return low + high[::-1]


def kernel(
    count_s,
    count_p,
    source_hbm,
    geometry_hbm,
    constant_hbm,
    matrix_hbm,
    solution_ref,
    residual_ref,
    source,
    geometry,
    constant,
    matrix,
    metric,
    fields,
    partial,
    planes,
    packs,
    packed,
    early,
    early_pack,
    own_side,
    far_side,
    face,
    response,
    grad1,
    grad2,
    row1,
    row2,
    result,
    column,
    plane,
    load_sem,
    send_sem,
    recv_sem,
    sum_send,
    sum_recv,
    side_sem,
):
    s, p, down, up, left, right = neighbours(count_s, count_p)
    core, _, _, z, base = place(s, p)
    gathers = z < HEADS
    block = X * Y * CORES
    long_down = lax.rem(s, block) == 0
    long_up = lax.rem(s, block) == block - 1
    is_long = long_down | long_up
    halo = [(down, p), (up, p), (s, left), (s, right)]
    halo += [(down, left), (down, right), (up, left), (up, right)]
    in_plane = plane_peers(s, p)
    heads = [(h, c) for h in range(HEADS) for c in range(CORES)]
    below = [
        in_column(base, lax.rem(z + dz, Z), lax.rem(core + dc, CORES))
        for dz in range(Z)
        for dc in range(CORES)
        if dz or dc
    ]

    loads = [
        pltpu.make_async_copy(source_hbm, source, load_sem.at[0]),
        pltpu.make_async_copy(constant_hbm, constant, load_sem.at[1]),
        pltpu.make_async_copy(geometry_hbm, geometry, load_sem.at[2]),
        pltpu.make_async_copy(matrix_hbm, matrix, load_sem.at[3]),
    ]
    barrier = pltpu.get_barrier_semaphore()
    for peer in halo:
        pl.semaphore_signal(barrier, inc=1, device_id=peer, device_id_type=MESH)
    for load in loads:
        load.start()

    @pl.when(gathers)
    def _():
        for peer in in_plane + below:
            pl.semaphore_signal(barrier, inc=1, device_id=peer, device_id_type=MESH)


    lane = lax.broadcasted_iota(jnp.int32, (NODES, LANES), 1)
    sub = lax.broadcasted_iota(jnp.int32, (NODES, LANES), 0)
    node = lax.rem(lane, NODES)
    from_right = (node == NODES - 1) & (lane != LANES - 1)
    from_left = (node == 0) & (lane != 0)

    def assemble(values, sums, pack_ref):
        tiles = [[values[x, 8 * e : 8 * e + 8] for e in range(EY)] for x in range(EX * NODES)]
        for e in range(EY):
            joined = tiles[NODES - 1][e] + tiles[NODES][e]
            tiles[NODES - 1][e] = tiles[NODES][e] = joined
        for x in range(EX * NODES):
            if x == NODES:
                for e in range(EY):
                    sums[x, 8 * e : 8 * e + 8, :] = tiles[NODES - 1][e]
                tiles[x] = tiles[NODES - 1]
                continue
            row = tiles[x]
            new = list(row)
            for e in range(EY - 1):
                new[e] = new[e] + jnp.where(sub == 7, pltpu.roll(row[e + 1], 7, 0), 0.0)
                new[e + 1] = new[e + 1] + jnp.where(sub == 0, pltpu.roll(row[e], 1, 0), 0.0)
            new[0] = jnp.where(sub == 0, 0.0, new[0])
            new[-1] = jnp.where(sub == 7, 0.0, new[-1])
            for e in range(EY):
                t = new[e]
                t = (
                    t
                    + jnp.where(from_right, pltpu.roll(t, LANES - 1, 1), 0.0)
                    + jnp.where(from_left, pltpu.roll(t, 1, 1), 0.0)
                )
                new[e] = t
                sums[x, 8 * e : 8 * e + 8, :] = t
            tiles[x] = new
        pack = jnp.zeros((NODES, LANES), jnp.float32)
        for x in range(EX * NODES):
            for e in range(EY):
                j = x * EY + e
                pack = jnp.where(lane // 2 == j, pltpu.roll(tiles[x][e], 2 * j + 1, 1), pack)
        pack_ref[...] = pack

    last = EX * NODES - 1

    def exchanges(k, sums=None, pack_ref=None):
        sums = partial.at[k] if sums is None else sums
        pack_ref = packed.at[k] if pack_ref is None else pack_ref
        sources = [sums.at[0], sums.at[last]] + [pack_ref] * 6
        targets = [planes.at[k, 1], planes.at[k, 0]]
        targets += [packs.at[k, i] for i in (1, 0, 5, 4, 3, 2)]
        slots = [1, 0, 3, 2, 7, 6, 5, 4]
        return [
            pltpu.make_async_remote_copy(
                src_ref=a,
                dst_ref=b,
                send_sem=send_sem.at[k, i],
                recv_sem=recv_sem.at[k, slots[i]],
                device_id=peer,
                device_id_type=MESH,
            )
            for i, (a, b, peer) in enumerate(zip(sources, targets, halo))
        ]

    def finish(k, want_norm, with_down=True, with_up=True):
        edge = EY * 2 * last
        low, high = lane < 2 * EY, (lane >= edge) & (lane < edge + 2 * EY)

        def with_corners(face, below, above):
            if with_down:
                face = face + jnp.where(low, pltpu.roll(packs[k, below], LANES - edge, 1), 0.0)
            if with_up:
                face = face + jnp.where(high, pltpu.roll(packs[k, above], edge, 1), 0.0)
            return face

        minus = with_corners(packs[k, 0], 2, 4)
        plus = with_corners(packs[k, 1], 3, 5)
        faces = jnp.where(
            lax.rem(lane, 2) == 0, pltpu.roll(plus, LANES - 1, 1), pltpu.roll(minus, 1, 1)
        )
        ends = (lane == 0) | (lane == LANES - 1)
        inner = jnp.zeros((NODES, LANES), jnp.float32)
        outer = jnp.zeros((NODES, LANES), jnp.float32)
        for x in range(EX * NODES):
            for e in range(EY):
                j = x * EY + e
                t = partial[k, x, 8 * e : 8 * e + 8, :]
                if x == 0 and with_down:
                    t = t + planes[k, 0, 8 * e : 8 * e + 8, :]
                if x == last and with_up:
                    t = t + planes[k, 1, 8 * e : 8 * e + 8, :]
                t = t + jnp.where(ends, pltpu.roll(faces, LANES - 2 * j - 1, 1), 0.0)
                fields[k, x, 8 * e : 8 * e + 8, :] = t
                if want_norm:
                    if x % NODES in (0, NODES - 1):
                        outer = outer + t * t
                    else:
                        inner = inner + t * t
        return (inner + 0.5 * outer) * constant[NODES : 2 * NODES, :]

    def fluxes(k):
        values = fields[k]
        parts = split(values.reshape(ROWS, LANES))
        grad2[...] = along_z(parts, (matrix[2], matrix[3])).reshape(values.shape)
        for r, group in enumerate(along_y(parts, (matrix[0], matrix[1]))):
            grad1[16 * r : 16 * r + 16] = group.reshape(16, NODES, LANES)
        energy = jnp.zeros((NODES, LANES), jnp.float32)
        flux0 = {}
        for ex in range(EX):
            for e in range(EY):
                rows = slice(8 * e, 8 * e + 8)
                g0 = along_x([fields[k, ex * 8 + i, rows, :] for i in range(8)], DERIVATIVE)
                for i in range(8):
                    x = ex * 8 + i
                    j = x * EY + e
                    m = [metric[c, x, rows, :] for c in range(6)]
                    g1, g2 = grad1[j], grad2[x, rows, :]
                    f0 = m[0] * g0[i] + m[3] * g1 + m[4] * g2
                    f1 = m[3] * g0[i] + m[1] * g1 + m[5] * g2
                    f2 = m[4] * g0[i] + m[5] * g1 + m[2] * g2
                    energy = energy + (f0 * g0[i] + f1 * g1 + f2 * g2)
                    flux0[x, e] = f0
                    grad1[j] = f1
                    grad2[x, rows, :] = f2
        return flux0, energy

    def divergence(flux0, add=False):
        flat = split(grad2[...].reshape(ROWS, LANES))
        along2 = along_z(flat, (matrix[0], matrix[1])).reshape(EX * NODES, EY * NODES, LANES)
        flat = split(grad1[...].reshape(ROWS, LANES))
        for r, group in enumerate(along_y(flat, (matrix[2], matrix[3]))):
            grad1[16 * r : 16 * r + 16] = group.reshape(16, NODES, LANES)
        total = {}
        for ex in range(EX):
            for e in range(EY):
                back = along_x([flux0[ex * 8 + i, e] for i in range(8)], DERIVATIVE.T)
                for i in range(8):
                    x = ex * 8 + i
                    total[x, e] = (
                        back[i] + grad1[x * EY + e] + along2[x, 8 * e : 8 * e + 8]
                    )
        if add:
            for e in range(EY):
                extra = response[8 * e : 8 * e + 8, :]
                total[0, e] = total[0, e] + jnp.where(long_down, extra, 0.0)
                total[last, e] = total[last, e] + jnp.where(long_up, extra, 0.0)
        return jnp.stack(
            [
                jnp.concatenate([total[x, e] for e in range(EY)], axis=0)
                for x in range(EX * NODES)
            ]
        )

    def side_copy():
        return pltpu.make_async_remote_copy(
            src_ref=own_side,
            dst_ref=far_side,
            send_sem=side_sem.at[0],
            recv_sem=side_sem.at[1],
            device_id=(jnp.where(long_down, down, up), p),
            device_id_type=MESH,
        )

    def describe_side(first, plane_index):
        squares = DERIVATIVE[:, 0 if first == 0 else NODES - 1] ** 2
        own_side[0] = sum(metric[0, first + i] * float(squares[i]) for i in range(NODES))
        for c in range(1, 6):
            own_side[c] = metric[c, plane_index]

    def respond():
        values = face[...]
        rest = jnp.zeros((LANES - EY * NODES, LANES), jnp.float32)
        slope = jnp.where(
            long_down, float(DERIVATIVE[NODES - 1, NODES - 1]), float(DERIVATIVE[0, 0])
        )

        def tall(v):
            return split(jnp.concatenate([v, rest], axis=0))

        parts = tall(values)
        d1 = along_y(parts, (matrix[0], matrix[1]))[0][: EY * NODES]
        d2 = along_z(parts, (matrix[2], matrix[3]))[: EY * NODES]
        d0 = slope * values
        f1 = far_side[3] * d0 + far_side[1] * d1 + far_side[5] * d2
        f2 = far_side[4] * d0 + far_side[5] * d1 + far_side[2] * d2
        response[...] = (
            far_side[0] * values
            + slope * (far_side[3] * d1 + far_side[4] * d2)
            + along_y(tall(f1), (matrix[2], matrix[3]))[0][: EY * NODES]
            + along_z(tall(f2), (matrix[0], matrix[1]))[: EY * NODES]
        )

    def fold(tile, width):
        shift = LANES // 2
        while shift >= width:
            tile = tile + pltpu.roll(tile, shift, 1)
            shift //= 2
        return tile

    loads[0].wait()
    assemble(source[...], partial.at[0], packed.at[0])
    pl.semaphore_wait(
        barrier,
        len(halo) + len(heads) + jnp.where(gathers, len(in_plane) - 1, 0),
    )
    flight = exchanges(0)
    for copy in flight:
        copy.start()
    loads[1].wait()
    loads[2].wait()
    loads[3].wait()
    weight = constant[0:NODES, :]
    for c in range(6):
        for x in range(EX * NODES):
            scaled = geometry[c, x].astype(jnp.float32)
            for e in range(EY):
                metric[c, x, 8 * e : 8 * e + 8, :] = scaled[8 * e : 8 * e + 8] * (
                    weight * float(WEIGHTS[x % NODES])
                )

    to_down, to_up = (0, 4, 5), (1, 6, 7)
    from_down, from_up = to_up, to_down

    def ahead(copies_from, copies_to, side_first, side_plane, **skip):
        describe_side(side_first, side_plane)
        side_copy().start()
        for i, copy in enumerate(flight):
            if i not in copies_from:
                copy.wait_recv()
        finish(0, False, **skip)
        face[...] = fields[0, side_plane]
        flux, _ = fluxes(0)
        assemble(divergence(flux), early, early_pack)
        for i, copy in enumerate(exchanges(1, early, early_pack)):
            if i in copies_to:
                copy.start()
        for i, copy in enumerate(flight):
            if i in copies_from:
                copy.wait_recv()

    @pl.when(long_down)
    def _():
        ahead(from_down, to_down, 0, 0, with_down=False)

    @pl.when(long_up)
    def _():
        ahead(from_up, to_up, NODES, last, with_up=False)

    @pl.when(jnp.logical_not(is_long))
    def _():
        for copy in flight:
            copy.wait_recv()

    moments = []
    for k in range(ROUNDS - 1):
        if k > 0:
            for copy in flight:
                copy.wait_recv()
        moments.append(finish(k, True))
        flux0, energy = fluxes(k)
        moments.append(energy)
        if k == ROUNDS - 2:
            packed_moments = jnp.where(
                lane < 96, fold(moments[4], 32), fold(moments[5], 32)
            )
            for i in range(4):
                packed_moments = jnp.where(
                    lane // 16 == i, fold(moments[i], 16), packed_moments
                )
            row1[...] = jnp.sum(packed_moments, axis=0, keepdims=True)
            for head, c in heads:
                offset = lax.rem(z + Z - head, Z) * CORES + lax.rem(core + CORES - c, CORES)

                @pl.when(offset > 0)
                def _(head=head, c=c, offset=offset):
                    pltpu.make_async_remote_copy(
                        src_ref=row1,
                        dst_ref=column.at[offset - 1],
                        send_sem=sum_send.at[0],
                        recv_sem=sum_recv.at[0],
                        device_id=in_column(base, jnp.int32(head), c),
                        device_id_type=MESH,
                    ).start()

        for copy in flight:
            copy.wait_send()
        if k == 0:

            @pl.when(is_long)
            def _():
                side_copy().wait_recv()
                respond()

        assemble(divergence(flux0, k == 0), partial.at[k + 1], packed.at[k + 1])
        flight = exchanges(k + 1)
        for i, copy in enumerate(flight):
            if k > 0 or i in (2, 3):
                copy.start()
            else:
                pl.when(jnp.logical_not(long_down if i in to_down else long_up))(copy.start)

    def whole(buffer, i):
        return pltpu.make_async_remote_copy(
            src_ref=buffer,
            dst_ref=buffer,
            send_sem=sum_send.at[i],
            recv_sem=sum_recv.at[i],
            device_id=halo[0],
            device_id_type=MESH,
        )

    @pl.when(gathers)
    def _():
        whole(column, 0).wait_recv()
        row2[...] = row1[...] + jnp.sum(column[...], axis=0)
        for i, peer in enumerate(in_plane):
            pltpu.make_async_remote_copy(
                src_ref=row2,
                dst_ref=plane.at[i],
                send_sem=sum_send.at[1],
                recv_sem=sum_recv.at[1],
                device_id=peer,
                device_id_type=MESH,
            ).start()

    for copy in flight:
        copy.wait_recv()
    finish(ROUNDS - 1, False)

    @pl.when(gathers)
    def _():
        whole(plane, 1).wait_recv()
        result[...] = row2[...] + jnp.sum(plane[...], axis=0)
        for i in range(FANOUT):
            target = jnp.where(z == 0, Z - 1 - i, HEADS + i)
            pltpu.make_async_remote_copy(
                src_ref=result,
                dst_ref=result,
                send_sem=sum_send.at[2],
                recv_sem=sum_recv.at[2],
                device_id=in_column(base, target, core),
                device_id_type=MESH,
            ).start()

    @pl.when(jnp.logical_not(gathers))
    def _():
        whole(result, 2).wait_recv()

    total = result[...]
    group = lax.broadcasted_iota(jnp.int32, (1, LANES), 1)
    bounds = [0, 16, 32, 48, 64, 96, 128]
    m = [
        jnp.sum(
            jnp.where((group >= bounds[i]) & (group < bounds[i + 1]), total, 0.0),
            axis=1,
            keepdims=True,
        )
        for i in range(6)
    ]
    alpha0 = m[0] / m[1]
    norm1 = alpha0 * alpha0 * m[2] - m[0]
    beta0 = norm1 / m[0]
    q = 1.0 + beta0
    alpha1 = norm1 / (q * q * m[1] - 2.0 * q * alpha0 * m[2] + alpha0 * alpha0 * m[3])
    r1, r2 = -(alpha0 + alpha1 * q), alpha0 * alpha1
    norm2 = (
        m[0]
        + 2.0 * r1 * m[1]
        + (r1 * r1 + 2.0 * r2) * m[2]
        + 2.0 * r1 * r2 * m[3]
        + r2 * r2 * m[4]
    )
    beta1 = norm2 / norm1
    d0, d1, d2 = 1.0 + beta1 * q, r1 - beta1 * alpha0, r2
    alpha2 = norm2 / (
        d0 * d0 * m[1]
        + 2.0 * d0 * d1 * m[2]
        + (d1 * d1 + 2.0 * d0 * d2) * m[3]
        + 2.0 * d1 * d2 * m[4]
        + d2 * d2 * m[5]
    )
    x0 = alpha0 + alpha1 * q + alpha2 * d0
    x1 = alpha2 * d1 - alpha1 * alpha0
    x2 = alpha2 * d2
    coefficients = [jnp.broadcast_to(v, (NODES, LANES)) for v in (x0, x1, x2)]
    for x in range(EX * NODES):
        for e in range(EY):
            rows = slice(8 * e, 8 * e + 8)
            v = [fields[k, x, rows, :] for k in range(ROUNDS)]
            solution_ref[x, rows, :] = (
                coefficients[0] * v[0] + coefficients[1] * v[1] + coefficients[2] * v[2]
            )
            residual_ref[x, rows, :] = v[0] - (
                coefficients[0] * v[1] + coefficients[1] * v[2] + coefficients[2] * v[3]
            )
    for copy in flight:
        copy.wait_send()

    @pl.when(is_long)
    def _():
        side_copy().wait_send()

    @pl.when(gathers)
    def _():
        whole(column.at[pl.ds(0, len(heads) - 1)], 0).wait_send()
        whole(plane, 1).wait_send()
        whole(column.at[pl.ds(0, FANOUT)], 2).wait_send()

    @pl.when(jnp.logical_not(gathers))
    def _():
        whole(column.at[pl.ds(0, len(heads))], 0).wait_send()


def store(a, b, a_out, b_out, sem):
    copies = [
        pltpu.make_async_copy(a, a_out, sem.at[0]),
        pltpu.make_async_copy(b, b_out, sem.at[1]),
    ]
    for copy in copies:
        copy.start()
    for copy in copies:
        copy.wait()


def solution(mesh):
    count_s, count_p = mesh.shape["stream"], mesh.shape["span"]

    def step(source, geometry):
        block = (EX * NODES, EY * NODES, LANES)
        in_hbm = pl.BlockSpec(memory_space=pltpu.HBM)
        f32 = jnp.float32
        pair = pl.pallas_call(
            functools.partial(kernel, count_s, count_p),
            out_shape=[pltpu.VMEM(block, f32)] * 2,
            in_specs=[in_hbm] * 4,
            out_specs=[pl.BlockSpec(memory_space=pltpu.VMEM)] * 2,
            scratch_shapes=[
                pltpu.VMEM(block, f32),
                pltpu.VMEM((6,) + block, jnp.bfloat16),
                pltpu.VMEM((2 * NODES, LANES), f32),
                pltpu.VMEM((4, LANES, LANES), jnp.bfloat16),
                pltpu.VMEM((6,) + block, f32),
                pltpu.VMEM((ROUNDS,) + block, f32),
                pltpu.VMEM((ROUNDS,) + block, f32),
                pltpu.VMEM((ROUNDS, 2) + block[1:], f32),
                pltpu.VMEM((ROUNDS, 6, NODES, LANES), f32),
                pltpu.VMEM((ROUNDS, NODES, LANES), f32),
                pltpu.VMEM(block, f32),
                pltpu.VMEM((NODES, LANES), f32),
                pltpu.VMEM((6,) + block[1:], f32),
                pltpu.VMEM((6,) + block[1:], f32),
                pltpu.VMEM(block[1:], f32),
                pltpu.VMEM(block[1:], f32),
                pltpu.VMEM((EX * NODES * EY, NODES, LANES), f32),
                pltpu.VMEM(block, f32),
                pltpu.VMEM((1, LANES), f32),
                pltpu.VMEM((1, LANES), f32),
                pltpu.VMEM((1, LANES), f32),
                pltpu.VMEM((Z * CORES - 1, 1, LANES), f32),
                pltpu.VMEM((X * Y - 1, 1, LANES), f32),
                pltpu.SemaphoreType.DMA((4,)),
                pltpu.SemaphoreType.DMA((ROUNDS, 8)),
                pltpu.SemaphoreType.DMA((ROUNDS, 8)),
                pltpu.SemaphoreType.DMA((3,)),
                pltpu.SemaphoreType.DMA((3,)),
                pltpu.SemaphoreType.DMA((2,)),
            ],
            compiler_params=pltpu.CompilerParams(
                collective_id=0, has_side_effects=True, vmem_limit_bytes=48 * 1024 * 1024
            ),
        )(*(pltpu.with_memory_space_constraint(v, pltpu.HBM) for v in (source, geometry, jnp.asarray(constants()), jnp.asarray(matrices()))))
        return pl.pallas_call(
            store,
            out_shape=[pltpu.HBM(block, f32)] * 2,
            in_specs=[pl.BlockSpec(memory_space=pltpu.VMEM)] * 2,
            out_specs=[in_hbm] * 2,
            scratch_shapes=[pltpu.SemaphoreType.DMA((2,))],
        )(*(pltpu.with_memory_space_constraint(v, pltpu.VMEM) for v in pair))

    return jax.shard_map(
        step,
        mesh=mesh,
        in_specs=(P("stream", None, "span"), P(None, "stream", None, "span")),
        out_specs=(P("stream", None, "span"), P("stream", None, "span")),
        check_vma=False,
    )
```

```python
import functools

import jax
import jax.numpy as jnp
import numpy as np
from jax import lax
from jax.experimental import pallas as pl
from jax.experimental.pallas import tpu as pltpu
from jax.sharding import PartitionSpec as P

MESH = pl.DeviceIdType.MESH
NODES = 8
EX = 2
EY = 3
LANES = 128
ROUNDS = 4
ROWS = EX * NODES * EY * NODES
Z_HI, X, Y, CORES, Z_LO = 3, 4, 8, 2, 4
Z = Z_HI * Z_LO
HEADS = 2
FANOUT = (Z - HEADS) // HEADS


def gll_tables():
    points = np.array(
        [
            -1.0,
            -0.8717401485096066,
            -0.5917001814331423,
            -0.2092992179024789,
            0.2092992179024789,
            0.5917001814331423,
            0.8717401485096066,
            1.0,
        ]
    )
    weights = np.array(
        [
            1.0 / 28.0,
            0.2107042271435061,
            0.3411226924835044,
            0.4124587946587038,
            0.4124587946587038,
            0.3411226924835044,
            0.2107042271435061,
            1.0 / 28.0,
        ]
    )
    barycentric = np.array(
        [
            1.0 / np.prod([points[j] - points[k] for k in range(8) if k != j])
            for j in range(8)
        ]
    )
    derivative = np.zeros((8, 8))
    for j in range(8):
        for k in range(8):
            if j != k:
                derivative[j, k] = barycentric[k] / barycentric[j] / (points[j] - points[k])
    for j in range(8):
        derivative[j, j] = -np.sum(derivative[j])
    return weights, derivative


WEIGHTS, DERIVATIVE = gll_tables()


def constants():
    half = np.ones(NODES)
    half[0] = half[-1] = 0.5
    copies = LANES // NODES
    weight = WEIGHTS[:, None] * np.tile(WEIGHTS, copies)[None, :]
    halves = half[:, None] * np.tile(half, copies)[None, :]
    return np.concatenate([weight, halves]).astype(np.float32)


def matrices():
    blocks = np.kron(np.eye(LANES // NODES), DERIVATIVE).astype(np.float32)
    parts = []
    for matrix in (blocks, blocks.T):
        lead = matrix.astype(jnp.bfloat16)
        parts += [lead, (matrix - lead.astype(np.float32)).astype(jnp.bfloat16)]
    return np.stack(parts)


def split(values):
    lead = values.astype(jnp.bfloat16)
    return lead, (values - lead.astype(jnp.float32)).astype(jnp.bfloat16)


def along_z(parts, matrix):
    wide = jnp.concatenate([matrix[0], matrix[1]], axis=1)
    product = jnp.dot(
        jnp.concatenate(parts, axis=1),
        jnp.concatenate([wide, wide], axis=0),
        preferred_element_type=jnp.float32,
    )
    return product[:, :LANES] + product[:, LANES:]


def along_y(parts, matrix):
    groups = parts[0].shape[0] // LANES
    tall = jnp.concatenate([matrix[0], matrix[1]], axis=0)
    stacked = [
        jnp.concatenate([part[LANES * r : LANES * r + LANES] for part in parts], axis=0)
        for r in range(groups)
    ]
    product = jnp.dot(
        jnp.concatenate([tall, tall], axis=1),
        jnp.concatenate(stacked, axis=1),
        preferred_element_type=jnp.float32,
    )
    product = product[:LANES] + product[LANES:]
    return [product[:, LANES * r : LANES * r + LANES] for r in range(groups)]


def neighbours(count_s, count_p):
    s, p = lax.axis_index("stream"), lax.axis_index("span")
    down, up = lax.rem(s + count_s - 1, count_s), lax.rem(s + 1, count_s)
    left, right = lax.rem(p + count_p - 1, count_p), lax.rem(p + 1, count_p)
    return s, p, down, up, left, right


def place(s, p):
    core, row = lax.rem(s, CORES), s // CORES
    y, x, z_hi = lax.rem(row, Y), lax.rem(row // Y, X), row // (X * Y)
    return core, x, y, z_hi * Z_LO + p, (x * Y + y) * CORES


def in_column(base, z, core):
    return base + (z // Z_LO) * (X * Y * CORES) + core, lax.rem(z, Z_LO)


def plane_peers(s, p):
    core, row = lax.rem(s, CORES), s // CORES
    y, x, z_hi = lax.rem(row, Y), lax.rem(row // Y, X), row // (X * Y)
    peers = []
    for dx in range(X):
        for dy in range(Y):
            if dx or dy:
                there = (z_hi * X + lax.rem(x + dx, X)) * Y + lax.rem(y + dy, Y)
                peers.append((there * CORES + core, p))
    return peers


def along_x(parts, matrix):
    even = [parts[j] + parts[7 - j] for j in range(4)]
    odd = [parts[j] - parts[7 - j] for j in range(4)]
    low, high = [None] * 4, [None] * 4
    for i in range(4):
        a = sum(odd[j] * float(0.5 * (matrix[i, j] - matrix[i, 7 - j])) for j in range(4))
        b = sum(even[j] * float(0.5 * (matrix[i, j] + matrix[i, 7 - j])) for j in range(4))
        low[i], high[i] = b + a, a - b
    return low + high[::-1]


def kernel(
    count_s,
    count_p,
    source_hbm,
    geometry_hbm,
    constant_hbm,
    matrix_hbm,
    solution_ref,
    residual_ref,
    source,
    geometry,
    constant,
    matrix,
    metric,
    fields,
    partial,
    planes,
    packs,
    packed,
    early,
    early_pack,
    own_side,
    far_side,
    face,
    response,
    grad1,
    grad2,
    row1,
    row2,
    result,
    column,
    plane,
    load_sem,
    send_sem,
    recv_sem,
    sum_send,
    sum_recv,
    side_sem,
):
    s, p, down, up, left, right = neighbours(count_s, count_p)
    core, _, _, z, base = place(s, p)
    gathers = z < HEADS
    block = X * Y * CORES
    long_down = lax.rem(s, block) == 0
    long_up = lax.rem(s, block) == block - 1
    is_long = long_down | long_up
    halo = [(down, p), (up, p), (s, left), (s, right)]
    halo += [(down, left), (down, right), (up, left), (up, right)]
    in_plane = plane_peers(s, p)
    heads = [(h, c) for h in range(HEADS) for c in range(CORES)]
    below = [
        in_column(base, lax.rem(z + dz, Z), lax.rem(core + dc, CORES))
        for dz in range(Z)
        for dc in range(CORES)
        if dz or dc
    ]

    loads = [
        pltpu.make_async_copy(source_hbm, source, load_sem.at[0]),
        pltpu.make_async_copy(constant_hbm, constant, load_sem.at[1]),
        pltpu.make_async_copy(geometry_hbm, geometry, load_sem.at[2]),
        pltpu.make_async_copy(matrix_hbm, matrix, load_sem.at[3]),
    ]
    barrier = pltpu.get_barrier_semaphore()
    for peer in halo:
        pl.semaphore_signal(barrier, inc=1, device_id=peer, device_id_type=MESH)
    for load in loads:
        load.start()

    @pl.when(gathers)
    def _():
        for peer in in_plane + below:
            pl.semaphore_signal(barrier, inc=1, device_id=peer, device_id_type=MESH)


    lane = lax.broadcasted_iota(jnp.int32, (NODES, LANES), 1)
    sub = lax.broadcasted_iota(jnp.int32, (NODES, LANES), 0)
    node = lax.rem(lane, NODES)
    from_right = (node == NODES - 1) & (lane != LANES - 1)
    from_left = (node == 0) & (lane != 0)

    def assemble(values, sums, pack_ref):
        tiles = [[values[x, 8 * e : 8 * e + 8] for e in range(EY)] for x in range(EX * NODES)]
        for e in range(EY):
            joined = tiles[NODES - 1][e] + tiles[NODES][e]
            tiles[NODES - 1][e] = tiles[NODES][e] = joined
        for x in range(EX * NODES):
            if x == NODES:
                for e in range(EY):
                    sums[x, 8 * e : 8 * e + 8, :] = tiles[NODES - 1][e]
                tiles[x] = tiles[NODES - 1]
                continue
            row = tiles[x]
            new = list(row)
            for e in range(EY - 1):
                new[e] = new[e] + jnp.where(sub == 7, pltpu.roll(row[e + 1], 7, 0), 0.0)
                new[e + 1] = new[e + 1] + jnp.where(sub == 0, pltpu.roll(row[e], 1, 0), 0.0)
            new[0] = jnp.where(sub == 0, 0.0, new[0])
            new[-1] = jnp.where(sub == 7, 0.0, new[-1])
            for e in range(EY):
                t = new[e]
                t = (
                    t
                    + jnp.where(from_right, pltpu.roll(t, LANES - 1, 1), 0.0)
                    + jnp.where(from_left, pltpu.roll(t, 1, 1), 0.0)
                )
                new[e] = t
                sums[x, 8 * e : 8 * e + 8, :] = t
            tiles[x] = new
        pack = jnp.zeros((NODES, LANES), jnp.float32)
        for x in range(EX * NODES):
            for e in range(EY):
                j = x * EY + e
                pack = jnp.where(lane // 2 == j, pltpu.roll(tiles[x][e], 2 * j + 1, 1), pack)
        pack_ref[...] = pack

    last = EX * NODES - 1

    def exchanges(k, sums=None, pack_ref=None):
        sums = partial.at[k] if sums is None else sums
        pack_ref = packed.at[k] if pack_ref is None else pack_ref
        sources = [sums.at[0], sums.at[last]] + [pack_ref] * 6
        targets = [planes.at[k, 1], planes.at[k, 0]]
        targets += [packs.at[k, i] for i in (1, 0, 5, 4, 3, 2)]
        slots = [1, 0, 3, 2, 7, 6, 5, 4]
        return [
            pltpu.make_async_remote_copy(
                src_ref=a,
                dst_ref=b,
                send_sem=send_sem.at[k, i],
                recv_sem=recv_sem.at[k, slots[i]],
                device_id=peer,
                device_id_type=MESH,
            )
            for i, (a, b, peer) in enumerate(zip(sources, targets, halo))
        ]

    def finish(k, want_norm, with_down=True, with_up=True):
        edge = EY * 2 * last
        low, high = lane < 2 * EY, (lane >= edge) & (lane < edge + 2 * EY)

        def with_corners(face, below, above):
            if with_down:
                face = face + jnp.where(low, pltpu.roll(packs[k, below], LANES - edge, 1), 0.0)
            if with_up:
                face = face + jnp.where(high, pltpu.roll(packs[k, above], edge, 1), 0.0)
            return face

        minus = with_corners(packs[k, 0], 2, 4)
        plus = with_corners(packs[k, 1], 3, 5)
        faces = jnp.where(
            lax.rem(lane, 2) == 0, pltpu.roll(plus, LANES - 1, 1), pltpu.roll(minus, 1, 1)
        )
        ends = (lane == 0) | (lane == LANES - 1)
        inner = jnp.zeros((NODES, LANES), jnp.float32)
        outer = jnp.zeros((NODES, LANES), jnp.float32)
        for x in range(EX * NODES):
            for e in range(EY):
                j = x * EY + e
                t = partial[k, x, 8 * e : 8 * e + 8, :]
                if x == 0 and with_down:
                    t = t + planes[k, 0, 8 * e : 8 * e + 8, :]
                if x == last and with_up:
                    t = t + planes[k, 1, 8 * e : 8 * e + 8, :]
                t = t + jnp.where(ends, pltpu.roll(faces, LANES - 2 * j - 1, 1), 0.0)
                fields[k, x, 8 * e : 8 * e + 8, :] = t
                if want_norm:
                    if x % NODES in (0, NODES - 1):
                        outer = outer + t * t
                    else:
                        inner = inner + t * t
        return (inner + 0.5 * outer) * constant[NODES : 2 * NODES, :]

    def fluxes(k):
        values = fields[k]
        parts = split(values.reshape(ROWS, LANES))
        grad2[...] = along_z(parts, (matrix[2], matrix[3])).reshape(values.shape)
        for r, group in enumerate(along_y(parts, (matrix[0], matrix[1]))):
            grad1[16 * r : 16 * r + 16] = group.reshape(16, NODES, LANES)
        energy = jnp.zeros((NODES, LANES), jnp.float32)
        flux0 = {}
        for ex in range(EX):
            for e in range(EY):
                rows = slice(8 * e, 8 * e + 8)
                g0 = along_x([fields[k, ex * 8 + i, rows, :] for i in range(8)], DERIVATIVE)
                for i in range(8):
                    x = ex * 8 + i
                    j = x * EY + e
                    m = [metric[c, x, rows, :] for c in range(6)]
                    g1, g2 = grad1[j], grad2[x, rows, :]
                    f0 = m[0] * g0[i] + m[3] * g1 + m[4] * g2
                    f1 = m[3] * g0[i] + m[1] * g1 + m[5] * g2
                    f2 = m[4] * g0[i] + m[5] * g1 + m[2] * g2
                    energy = energy + (f0 * g0[i] + f1 * g1 + f2 * g2)
                    flux0[x, e] = f0
                    grad1[j] = f1
                    grad2[x, rows, :] = f2
        return flux0, energy

    def divergence(flux0, answer=None):
        flat = split(grad2[...].reshape(ROWS, LANES))
        along2 = along_z(flat, (matrix[0], matrix[1])).reshape(EX * NODES, EY * NODES, LANES)
        flat = split(grad1[...].reshape(ROWS, LANES))
        for r, group in enumerate(along_y(flat, (matrix[2], matrix[3]))):
            grad1[16 * r : 16 * r + 16] = group.reshape(16, NODES, LANES)
        total = {}
        for ex in range(EX):
            for e in range(EY):
                back = along_x([flux0[ex * 8 + i, e] for i in range(8)], DERIVATIVE.T)
                for i in range(8):
                    x = ex * 8 + i
                    total[x, e] = (
                        back[i] + grad1[x * EY + e] + along2[x, 8 * e : 8 * e + 8]
                    )
        if answer is not None:
            answer()
            for e in range(EY):
                extra = response[8 * e : 8 * e + 8, :]
                total[0, e] = total[0, e] + jnp.where(long_down, extra, 0.0)
                total[last, e] = total[last, e] + jnp.where(long_up, extra, 0.0)
        return jnp.stack(
            [
                jnp.concatenate([total[x, e] for e in range(EY)], axis=0)
                for x in range(EX * NODES)
            ]
        )

    def side_copy():
        return pltpu.make_async_remote_copy(
            src_ref=own_side,
            dst_ref=far_side,
            send_sem=side_sem.at[0],
            recv_sem=side_sem.at[1],
            device_id=(jnp.where(long_down, down, up), p),
            device_id_type=MESH,
        )

    def describe_side(first, plane_index):
        squares = DERIVATIVE[:, 0 if first == 0 else NODES - 1] ** 2
        own_side[0] = sum(metric[0, first + i] * float(squares[i]) for i in range(NODES))
        for c in range(1, 6):
            own_side[c] = metric[c, plane_index]

    def respond():
        values = face[...]
        rest = jnp.zeros((LANES - EY * NODES, LANES), jnp.float32)
        slope = jnp.where(
            long_down, float(DERIVATIVE[NODES - 1, NODES - 1]), float(DERIVATIVE[0, 0])
        )

        def tall(v):
            return split(jnp.concatenate([v, rest], axis=0))

        parts = tall(values)
        d1 = along_y(parts, (matrix[0], matrix[1]))[0][: EY * NODES]
        d2 = along_z(parts, (matrix[2], matrix[3]))[: EY * NODES]
        d0 = slope * values
        f1 = far_side[3] * d0 + far_side[1] * d1 + far_side[5] * d2
        f2 = far_side[4] * d0 + far_side[5] * d1 + far_side[2] * d2
        response[...] = (
            far_side[0] * values
            + slope * (far_side[3] * d1 + far_side[4] * d2)
            + along_y(tall(f1), (matrix[2], matrix[3]))[0][: EY * NODES]
            + along_z(tall(f2), (matrix[0], matrix[1]))[: EY * NODES]
        )

    def fold(tile, width):
        shift = LANES // 2
        while shift >= width:
            tile = tile + pltpu.roll(tile, shift, 1)
            shift //= 2
        return tile

    loads[0].wait()
    assemble(source[...], partial.at[0], packed.at[0])
    loads[1].wait()
    loads[2].wait()
    loads[3].wait()
    weight = constant[0:NODES, :]
    for c in range(6):
        for x in range(EX * NODES):
            scaled = geometry[c, x].astype(jnp.float32)
            for e in range(EY):
                metric[c, x, 8 * e : 8 * e + 8, :] = scaled[8 * e : 8 * e + 8] * (
                    weight * float(WEIGHTS[x % NODES])
                )


    @pl.when(long_down)
    def _():
        describe_side(0, 0)

    @pl.when(long_up)
    def _():
        describe_side(NODES, last)

    pl.semaphore_wait(
        barrier,
        len(halo) + len(heads) + jnp.where(gathers, len(in_plane) - 1, 0),
    )
    flight = exchanges(0)
    for copy in flight[::-1]:
        copy.start()
    pl.when(is_long)(side_copy().start)
    to_down, to_up = (0, 4, 5), (1, 6, 7)
    from_down, from_up = to_up, to_down

    def ahead(copies_from, copies_to, side_first, side_plane, **skip):
        for i, copy in enumerate(flight):
            if i not in copies_from:
                copy.wait_recv()
        finish(0, False, **skip)
        face[...] = fields[0, side_plane]
        flux, _ = fluxes(0)
        assemble(divergence(flux), early, early_pack)
        for i, copy in list(enumerate(exchanges(1, early, early_pack)))[::-1]:
            if i in copies_to:
                copy.start()
        for i, copy in enumerate(flight):
            if i in copies_from:
                copy.wait_recv()

    @pl.when(long_down)
    def _():
        ahead(from_down, to_down, 0, 0, with_down=False)

    @pl.when(long_up)
    def _():
        ahead(from_up, to_up, NODES, last, with_up=False)

    @pl.when(jnp.logical_not(is_long))
    def _():
        for copy in flight:
            copy.wait_recv()

    def answer():
        @pl.when(is_long)
        def _():
            side_copy().wait_recv()
            respond()

    moments = []
    for k in range(ROUNDS - 1):
        if k > 0:
            for copy in flight:
                copy.wait_recv()
        moments.append(finish(k, True))
        flux0, energy = fluxes(k)
        moments.append(energy)
        if k == ROUNDS - 2:
            packed_moments = jnp.where(
                lane < 96, fold(moments[4], 32), fold(moments[5], 32)
            )
            for i in range(4):
                packed_moments = jnp.where(
                    lane // 16 == i, fold(moments[i], 16), packed_moments
                )
            row1[...] = jnp.sum(packed_moments, axis=0, keepdims=True)
            for head, c in heads:
                offset = lax.rem(z + Z - head, Z) * CORES + lax.rem(core + CORES - c, CORES)

                @pl.when(offset > 0)
                def _(head=head, c=c, offset=offset):
                    pltpu.make_async_remote_copy(
                        src_ref=row1,
                        dst_ref=column.at[offset - 1],
                        send_sem=sum_send.at[0],
                        recv_sem=sum_recv.at[0],
                        device_id=in_column(base, jnp.int32(head), c),
                        device_id_type=MESH,
                    ).start()

        for copy in flight:
            copy.wait_send()
        values = divergence(flux0, answer if k == 0 else None)
        assemble(values, partial.at[k + 1], packed.at[k + 1])
        flight = exchanges(k + 1)
        for i, copy in list(enumerate(flight))[::-1]:
            if k > 0 or i in (2, 3):
                copy.start()
            else:
                pl.when(jnp.logical_not(long_down if i in to_down else long_up))(copy.start)

    def whole(buffer, i):
        return pltpu.make_async_remote_copy(
            src_ref=buffer,
            dst_ref=buffer,
            send_sem=sum_send.at[i],
            recv_sem=sum_recv.at[i],
            device_id=halo[0],
            device_id_type=MESH,
        )

    @pl.when(gathers)
    def _():
        whole(column, 0).wait_recv()
        row2[...] = row1[...] + jnp.sum(column[...], axis=0)
        for i, peer in enumerate(in_plane):
            pltpu.make_async_remote_copy(
                src_ref=row2,
                dst_ref=plane.at[i],
                send_sem=sum_send.at[1],
                recv_sem=sum_recv.at[1],
                device_id=peer,
                device_id_type=MESH,
            ).start()

    for copy in flight:
        copy.wait_recv()
    finish(ROUNDS - 1, False)

    @pl.when(gathers)
    def _():
        whole(plane, 1).wait_recv()
        result[...] = row2[...] + jnp.sum(plane[...], axis=0)
        for i in range(FANOUT):
            target = jnp.where(z == 0, Z - 1 - i, HEADS + i)
            pltpu.make_async_remote_copy(
                src_ref=result,
                dst_ref=result,
                send_sem=sum_send.at[2],
                recv_sem=sum_recv.at[2],
                device_id=in_column(base, target, core),
                device_id_type=MESH,
            ).start()

    @pl.when(jnp.logical_not(gathers))
    def _():
        whole(result, 2).wait_recv()

    total = result[...]
    group = lax.broadcasted_iota(jnp.int32, (1, LANES), 1)
    bounds = [0, 16, 32, 48, 64, 96, 128]
    m = [
        jnp.sum(
            jnp.where((group >= bounds[i]) & (group < bounds[i + 1]), total, 0.0),
            axis=1,
            keepdims=True,
        )
        for i in range(6)
    ]
    alpha0 = m[0] / m[1]
    norm1 = alpha0 * alpha0 * m[2] - m[0]
    beta0 = norm1 / m[0]
    q = 1.0 + beta0
    alpha1 = norm1 / (q * q * m[1] - 2.0 * q * alpha0 * m[2] + alpha0 * alpha0 * m[3])
    r1, r2 = -(alpha0 + alpha1 * q), alpha0 * alpha1
    norm2 = (
        m[0]
        + 2.0 * r1 * m[1]
        + (r1 * r1 + 2.0 * r2) * m[2]
        + 2.0 * r1 * r2 * m[3]
        + r2 * r2 * m[4]
    )
    beta1 = norm2 / norm1
    d0, d1, d2 = 1.0 + beta1 * q, r1 - beta1 * alpha0, r2
    alpha2 = norm2 / (
        d0 * d0 * m[1]
        + 2.0 * d0 * d1 * m[2]
        + (d1 * d1 + 2.0 * d0 * d2) * m[3]
        + 2.0 * d1 * d2 * m[4]
        + d2 * d2 * m[5]
    )
    x0 = alpha0 + alpha1 * q + alpha2 * d0
    x1 = alpha2 * d1 - alpha1 * alpha0
    x2 = alpha2 * d2
    coefficients = [jnp.broadcast_to(v, (NODES, LANES)) for v in (x0, x1, x2)]
    for x in range(EX * NODES):
        for e in range(EY):
            rows = slice(8 * e, 8 * e + 8)
            v = [fields[k, x, rows, :] for k in range(ROUNDS)]
            solution_ref[x, rows, :] = (
                coefficients[0] * v[0] + coefficients[1] * v[1] + coefficients[2] * v[2]
            )
            residual_ref[x, rows, :] = v[0] - (
                coefficients[0] * v[1] + coefficients[1] * v[2] + coefficients[2] * v[3]
            )
    for copy in flight:
        copy.wait_send()

    @pl.when(is_long)
    def _():
        side_copy().wait_send()

    @pl.when(gathers)
    def _():
        whole(column.at[pl.ds(0, len(heads) - 1)], 0).wait_send()
        whole(plane, 1).wait_send()
        whole(column.at[pl.ds(0, FANOUT)], 2).wait_send()

    @pl.when(jnp.logical_not(gathers))
    def _():
        whole(column.at[pl.ds(0, len(heads))], 0).wait_send()


def store(a, b, a_out, b_out, sem):
    copies = [
        pltpu.make_async_copy(a, a_out, sem.at[0]),
        pltpu.make_async_copy(b, b_out, sem.at[1]),
    ]
    for copy in copies:
        copy.start()
    for copy in copies:
        copy.wait()


def solution(mesh):
    count_s, count_p = mesh.shape["stream"], mesh.shape["span"]

    def step(source, geometry):
        block = (EX * NODES, EY * NODES, LANES)
        in_hbm = pl.BlockSpec(memory_space=pltpu.HBM)
        f32 = jnp.float32
        pair = pl.pallas_call(
            functools.partial(kernel, count_s, count_p),
            out_shape=[pltpu.VMEM(block, f32)] * 2,
            in_specs=[in_hbm] * 4,
            out_specs=[pl.BlockSpec(memory_space=pltpu.VMEM)] * 2,
            scratch_shapes=[
                pltpu.VMEM(block, f32),
                pltpu.VMEM((6,) + block, jnp.bfloat16),
                pltpu.VMEM((2 * NODES, LANES), f32),
                pltpu.VMEM((4, LANES, LANES), jnp.bfloat16),
                pltpu.VMEM((6,) + block, f32),
                pltpu.VMEM((ROUNDS,) + block, f32),
                pltpu.VMEM((ROUNDS,) + block, f32),
                pltpu.VMEM((ROUNDS, 2) + block[1:], f32),
                pltpu.VMEM((ROUNDS, 6, NODES, LANES), f32),
                pltpu.VMEM((ROUNDS, NODES, LANES), f32),
                pltpu.VMEM(block, f32),
                pltpu.VMEM((NODES, LANES), f32),
                pltpu.VMEM((6,) + block[1:], f32),
                pltpu.VMEM((6,) + block[1:], f32),
                pltpu.VMEM(block[1:], f32),
                pltpu.VMEM(block[1:], f32),
                pltpu.VMEM((EX * NODES * EY, NODES, LANES), f32),
                pltpu.VMEM(block, f32),
                pltpu.VMEM((1, LANES), f32),
                pltpu.VMEM((1, LANES), f32),
                pltpu.VMEM((1, LANES), f32),
                pltpu.VMEM((Z * CORES - 1, 1, LANES), f32),
                pltpu.VMEM((X * Y - 1, 1, LANES), f32),
                pltpu.SemaphoreType.DMA((4,)),
                pltpu.SemaphoreType.DMA((ROUNDS, 8)),
                pltpu.SemaphoreType.DMA((ROUNDS, 8)),
                pltpu.SemaphoreType.DMA((3,)),
                pltpu.SemaphoreType.DMA((3,)),
                pltpu.SemaphoreType.DMA((2,)),
            ],
            compiler_params=pltpu.CompilerParams(
                collective_id=0, has_side_effects=True, vmem_limit_bytes=48 * 1024 * 1024
            ),
        )(*(pltpu.with_memory_space_constraint(v, pltpu.HBM) for v in (source, geometry, jnp.asarray(constants()), jnp.asarray(matrices()))))
        return pl.pallas_call(
            store,
            out_shape=[pltpu.HBM(block, f32)] * 2,
            in_specs=[pl.BlockSpec(memory_space=pltpu.VMEM)] * 2,
            out_specs=[in_hbm] * 2,
            scratch_shapes=[pltpu.SemaphoreType.DMA((2,))],
        )(*(pltpu.with_memory_space_constraint(v, pltpu.VMEM) for v in pair))

    return jax.shard_map(
        step,
        mesh=mesh,
        in_specs=(P("stream", None, "span"), P(None, "stream", None, "span")),
        out_specs=(P("stream", None, "span"), P("stream", None, "span")),
        check_vma=False,
    )
```
